128 devices in a mesh: row: 4 (over y), col: 8 (over x_hi, z), ch: 4 (over x_lo, core).
Axes of the slice: x: 4 (x_hi: 2, x_lo: 2; x = x_hi * 2 + x_lo), y: 4, z: 4, core: 2. Of those that a mesh axis runs over, the one named last changes fastest.
Arguments:
- pair_tensor: bfloat16 [128, 1024, 1024], P('ch', 'row', 'col'), may hold values from -6 to 6
- token_mask: int32 [1024], replicated, may hold values 0 or 1
- norm_in_gain: float32 [128], replicated, may hold values from 0.5 to 1.5
- norm_in_bias: float32 [128], replicated, may hold values from -3 to 3
- proj_in: bfloat16 [128, 256], replicated, may hold values from -0.5 to 0.5
- gate_in: bfloat16 [128, 256], replicated, may hold values from -0.5 to 0.5
- norm_out_gain: float32 [128], replicated, may hold values from 0.5 to 1.5
- norm_out_bias: float32 [128], replicated, may hold values from -3 to 3
- proj_out: bfloat16 [128, 128], replicated, may hold values from -0.5 to 0.5
- gate_out: bfloat16 [128, 128], replicated, may hold values from -0.5 to 0.5
Outputs:
- update: bfloat16 [128, 1024, 1024], P('ch', 'row', 'col')
The draws below stay inside these ranges and needn't reach their ends.
All inputs are finite; a program needn't handle non-finite values.
Results may differ from the reference program's by a relative error of at most 0.005.
Values may be sent and summed in bfloat16 or wider, within the bound.
A program may use at most 192 MiB of HBM per device.

```python
import jax
import jax.numpy as jnp
from jax import lax

C = 128
H = 128
N = 1024


def with_ends(values, key, smallest, largest):
    dims = values.shape
    place = [jax.random.randint(jax.random.fold_in(key, axis), (), 0, dims[axis]) for axis in range(len(dims))]
    values = values.at[tuple(place)].set(smallest)
    longest = dims.index(max(dims))
    place[longest] = (place[longest] + 1) % dims[longest]
    return values.at[tuple(place)].set(largest)


def block_scale(own_key, shape, pieces, least, largest):
    gain = 1.0
    for position, parts in pieces:
        draws = jax.random.uniform(jax.random.fold_in(jax.random.fold_in(own_key, 6), position), (parts,), jnp.float32, least / len(pieces), largest / len(pieces))
        gain = gain * jnp.repeat(jnp.exp(draws), shape[position] // parts).reshape((-1,) + (1,) * (len(shape) - 1 - position))
    return gain


def gaussian(rng, extent, width, limit, split=(), dtype=jnp.bfloat16):
    values = jax.random.normal(rng, extent, jnp.float32) * width
    if len(split) > 0:
        values = block_scale(rng, extent, split, -0.22, 0.18) * values
    return jnp.clip(values, min=-limit, max=limit).astype(dtype)


def setup_inputs(seed: int = 0) -> dict:
    key_list = jax.random.split(jax.random.key(seed), 11)
    return {
        "pair_tensor": gaussian(key_list[0], (C, N, N), 1.0, 6.0, ((0, 4), (1, 4), (2, 8))),
        "token_mask": with_ends((jax.random.randint(key_list[1], (N,), 0, 8) < 7).astype(jnp.int32), jax.random.fold_in(key_list[1], 1), 0, 1),
        "norm_in_gain": jnp.clip(jax.random.uniform(key_list[2], (C,), jnp.float32, 0.5, 1.5), 0.5, 1.5),
        "norm_in_bias": gaussian(key_list[3], (C,), 0.5, 3.0, (), jnp.float32),
        "proj_in": gaussian(key_list[4], (C, 2 * H), C ** -0.5, 0.5),
        "gate_in": gaussian(key_list[5], (C, 2 * H), C ** -0.5, 0.5),
        "norm_out_gain": jnp.clip(jax.random.uniform(key_list[6], (H,), jnp.float32, 0.5, 1.5), 0.5, 1.5),
        "norm_out_bias": gaussian(key_list[7], (H,), 0.5, 3.0, (), jnp.float32),
        "proj_out": gaussian(key_list[8], (H, C), H ** -0.5, 0.5),
        "gate_out": gaussian(key_list[9], (C, C), C ** -0.5, 0.5),
    }


epsilon = 1e-05

def layer_norm(values, gain_vec, bias_vec):
    center = lax.optimization_barrier(jnp.mean(values, axis=-1, keepdims=True))
    second = lax.optimization_barrier(jnp.mean(values * values, axis=-1, keepdims=True))
    spread = second - center * center
    return (values - center) * lax.rsqrt(spread + epsilon) * gain_vec + bias_vec

def reference(pair_tensor, token_mask, norm_in_gain, norm_in_bias, proj_in, gate_in, norm_out_gain, norm_out_bias, proj_out, gate_out):
    pair_last = jnp.transpose(pair_tensor, (1, 2, 0))
    normed = layer_norm(pair_last.astype(jnp.float32), norm_in_gain, norm_in_bias).astype(jnp.bfloat16)
    mask_f = token_mask.astype(jnp.float32)
    pair_mask = mask_f[:, None] * mask_f[None, :]
    proj_val = jnp.dot(normed, proj_in, preferred_element_type=jnp.float32)
    gate_val = jnp.dot(normed, gate_in, preferred_element_type=jnp.float32)
    hidden_act = (jax.nn.sigmoid(gate_val) * proj_val * pair_mask[:, :, None]).astype(jnp.bfloat16)
    left_act = hidden_act[:, :, :H].astype(jnp.float32)
    right_act = hidden_act[:, :, H:].astype(jnp.float32)
    tri_sum = jnp.einsum('ikh,jkh->ijh', left_act, right_act, precision=lax.Precision.HIGHEST)
    tri_norm = layer_norm(tri_sum, norm_out_gain, norm_out_bias).astype(jnp.bfloat16)
    out_val = jnp.dot(tri_norm, proj_out, preferred_element_type=jnp.float32)
    out_gate = jnp.dot(normed, gate_out, preferred_element_type=jnp.float32)
    result = (jax.nn.sigmoid(out_gate) * out_val).astype(jnp.bfloat16)
    return jnp.transpose(result, (2, 0, 1))
```

```python
import functools

import jax
import jax.numpy as jnp
from jax import lax
from jax.experimental import pallas as pl
from jax.experimental.pallas import tpu as pltpu
from jax.sharding import PartitionSpec as P

epsilon = 1e-05
WORLD = ("row", "col", "ch")
STEP = 16


def norm_rows(values, gain, bias):
    width = values.shape[0]
    center = jnp.sum(values, axis=0, keepdims=True) * (1.0 / width)
    second = jnp.sum(values * values, axis=0, keepdims=True) * (1.0 / width)
    spread = second - center * center
    return ((values - center) * lax.rsqrt(spread + epsilon) * gain + bias).astype(jnp.bfloat16)


def sigmoid(values):
    return 0.5 * jnp.tanh(0.5 * values) + 0.5


def hidden_kernel(pair_ref, mask_ref, gain_ref, bias_ref, weight_ref, hid_ref, gate_ref, flat, acts):
    chans, _, lanes = pair_ref.shape
    hid2 = 2 * hid_ref.shape[0]
    flat[...] = pair_ref[...].astype(jnp.float32).reshape(chans * STEP, lanes)
    gain, bias = gain_ref[...], bias_ref[...]
    weight = weight_ref[...]
    for i in range(0, STEP, 2):
        both = [norm_rows(flat[pl.ds(i + d, chans, stride=STEP), :], gain, bias) for d in range(2)]
        prod = jnp.dot(weight, jnp.concatenate(both, axis=1), preferred_element_type=jnp.float32)
        for d in range(2):
            part = prod[:, d * lanes : (d + 1) * lanes]
            act = sigmoid(part[:hid2]) * part[hid2 : 2 * hid2] * mask_ref[i + d : i + d + 1, :]
            acts[pl.ds(i + d, hid2, stride=STEP), :] = act
            gate_ref[i + d] = sigmoid(part[2 * hid2 :])
    rounded = acts[...].astype(jnp.bfloat16).reshape(hid2, STEP, lanes)
    hid_ref[:, 0] = rounded[: hid2 // 2]
    hid_ref[:, 1] = rounded[hid2 // 2 :]


def triangle_kernel(recv_ref, out_ref, left, right):
    rows, cols, chs, _, tall, lanes = recv_ref.shape
    for r in range(rows):
        for h in range(chs):
            for c in range(cols):
                at = (pl.ds((r * chs + h) * tall, tall), pl.ds(c * lanes, lanes))
                left[at] = recv_ref[r, c, h, 0]
                right[at] = recv_ref[r, c, h, 1]
    for r in range(rows):
        prod = lax.dot_general(
            left[pl.ds(r * chs * tall, chs * tall), :],
            right[...],
            (((1,), (1,)), ((), ())),
            preferred_element_type=jnp.float32,
        ).astype(jnp.bfloat16)
        for h in range(chs):
            for c in range(cols):
                out_ref[r, c, h] = prod[h * tall : (h + 1) * tall, c * lanes : (c + 1) * lanes]


def update_kernel(tri_ref, gate_ref, gain_ref, bias_ref, weight_ref, out_ref, flat, outs):
    hids, _, lanes = tri_ref.shape
    chans = out_ref.shape[0]
    flat[...] = tri_ref[...].astype(jnp.float32).reshape(hids * STEP, lanes)
    gain, bias = gain_ref[...], bias_ref[...]
    weight = weight_ref[...]
    for i in range(0, STEP, 2):
        both = [norm_rows(flat[pl.ds(i + d, hids, stride=STEP), :], gain, bias) for d in range(2)]
        prod = jnp.dot(weight, jnp.concatenate(both, axis=1), preferred_element_type=jnp.float32)
        for d in range(2):
            outs[pl.ds(i + d, chans, stride=STEP), :] = gate_ref[i + d] * prod[:, d * lanes : (d + 1) * lanes]
    out_ref[...] = outs[...].astype(jnp.bfloat16).reshape(chans, STEP, lanes)


def whole(shape):
    return pl.BlockSpec(shape, lambda i: (0,) * len(shape))


def local(pair, token_mask, gain_in, bias_in, proj_in, gate_in, gain_out, bias_out, proj_out, gate_out):
    chan_part, row_count, lanes = pair.shape
    rows, cols, chs = (lax.axis_size(a) for a in WORLD)
    chans, hids = chan_part * chs, proj_out.shape[0]
    world = rows * cols * chs
    tall = row_count // chs
    row_start = lax.axis_index("row") * row_count + lax.axis_index("ch") * tall
    col_start = lax.axis_index("col") * lanes
    row_mask = lax.dynamic_slice_in_dim(token_mask, row_start, tall, 0).astype(jnp.float32)
    col_mask = lax.dynamic_slice_in_dim(token_mask, col_start, lanes, 0).astype(jnp.float32)
    mask = row_mask[:, None] * col_mask[None, :]
    wide = lambda v: jnp.broadcast_to(v[:, None], (v.shape[0], lanes))
    weight = jnp.concatenate([gate_in, proj_in, gate_out], axis=1).T
    params = pltpu.CompilerParams(vmem_limit_bytes=48 * 2**20)

    mine = lax.all_to_all(pair, "ch", 1, 0, tiled=True)
    hid, gate = pl.pallas_call(
        hidden_kernel,
        name="hidden",
        grid=(tall // STEP,),
        out_shape=(
            jax.ShapeDtypeStruct((hids, 2, tall, lanes), jnp.bfloat16),
            jax.ShapeDtypeStruct((tall, chans, lanes), jnp.float32),
        ),
        in_specs=[
            pl.BlockSpec((chans, STEP, lanes), lambda i: (0, i, 0)),
            pl.BlockSpec((STEP, lanes), lambda i: (i, 0)),
            whole((chans, lanes)),
            whole((chans, lanes)),
            whole(weight.shape),
        ],
        out_specs=(
            pl.BlockSpec((hids, 2, STEP, lanes), lambda i: (0, 0, i, 0)),
            pl.BlockSpec((STEP, chans, lanes), lambda i: (i, 0, 0)),
        ),
        scratch_shapes=[
            pltpu.VMEM((chans * STEP, lanes), jnp.float32),
            pltpu.VMEM((2 * hids * STEP, lanes), jnp.float32),
        ],
        compiler_params=params,
    )(mine, mask, wide(gain_in), wide(bias_in), weight)
    recv = lax.all_to_all(hid, WORLD, 0, 0, tiled=True).reshape(rows, cols, chs, 2, tall, lanes)
    tri = pl.pallas_call(
        triangle_kernel,
        name="triangle",
        out_shape=jax.ShapeDtypeStruct((rows, cols, chs, tall, lanes), jnp.bfloat16),
        scratch_shapes=[pltpu.VMEM((rows * row_count, cols * lanes), jnp.bfloat16)] * 2,
        compiler_params=params,
    )(recv)
    sums = lax.all_to_all(tri.reshape(world, tall, lanes), WORLD, 0, 0, tiled=True)
    weight_out = proj_out.T
    out = pl.pallas_call(
        update_kernel,
        name="update",
        grid=(tall // STEP,),
        out_shape=jax.ShapeDtypeStruct((chans, tall, lanes), jnp.bfloat16),
        in_specs=[
            pl.BlockSpec((hids, STEP, lanes), lambda i: (0, i, 0)),
            pl.BlockSpec((STEP, chans, lanes), lambda i: (i, 0, 0)),
            whole((hids, lanes)),
            whole((hids, lanes)),
            whole(weight_out.shape),
        ],
        out_specs=pl.BlockSpec((chans, STEP, lanes), lambda i: (0, i, 0)),
        scratch_shapes=[
            pltpu.VMEM((hids * STEP, lanes), jnp.float32),
            pltpu.VMEM((chans * STEP, lanes), jnp.float32),
        ],
        compiler_params=params,
    )(sums, gate, wide(gain_out), wide(bias_out), weight_out)
    return lax.all_to_all(out, "ch", 0, 1, tiled=True)


def solution(mesh):
    in_specs = (P("ch", "row", "col"),) + (P(),) * 9
    return jax.shard_map(local, mesh=mesh, in_specs=in_specs, out_specs=P("ch", "row", "col"), check_vma=False)
```

```python
import functools

import jax
import jax.numpy as jnp
from jax import lax
from jax.experimental import pallas as pl
from jax.experimental.pallas import tpu as pltpu
from jax.sharding import PartitionSpec as P

epsilon = 1e-05
MESH = pl.DeviceIdType.MESH
STEP = 16
PARTS = 4
ROUNDS = 2
PER = PARTS // ROUNDS
LANES = 128
PEERS = 64


def norm_rows(values, gain, bias):
    width = values.shape[0]
    center = jnp.sum(values, axis=0, keepdims=True) * (1.0 / width)
    second = jnp.sum(values * values, axis=0, keepdims=True) * (1.0 / width)
    spread = second - center * center
    return ((values - center) * lax.rsqrt(spread + epsilon) * gain + bias).astype(jnp.bfloat16)


def sigmoid(values):
    return 0.5 * jnp.tanh(0.5 * values) + 0.5


def part_rows(r):
    return pl.ds(pl.multiple_of(r * STEP, STEP), STEP)


def kernel(
    pair_ref,
    mask_ref,
    gain_in_ref,
    bias_in_ref,
    weight_in_ref,
    gain_out_ref,
    bias_out_ref,
    weight_out_ref,
    out_ref,
    pairs,
    hidden,
    gates,
    acts,
    far,
    tri,
    sums,
    result,
    flat,
    stage,
    send_sem,
    pair_sem,
    act_sem,
    far_sem,
    sum_sem,
    out_sem,
    own_pair_sem,
    own_act_sem,
    own_sum_sem,
    own_out_sem,
):
    y, col, ch = lax.axis_index("row"), lax.axis_index("col"), lax.axis_index("ch")
    b, z = lax.div(col, 4), lax.rem(col, 4)
    low, core = lax.div(ch, 2), lax.rem(ch, 2)
    half = lax.rem(low + b, 2)
    quarter = half * 2 + core
    chan_part = pair_ref.shape[0]
    tall = STEP * PARTS

    def place(b2, y2, z2, core2):
        return {"row": y2, "col": b2 * 4 + z2, "ch": lax.rem(half + b2, 2) * 2 + core2}

    def group(b2, y2, z2, core2):
        return ((b2 * 4 + y2) * 4 + z2) * 2 + core2

    def peer(t):
        k = lax.rem(t * 37, PEERS)
        return (
            lax.rem(b + lax.div(k, 32), 2),
            lax.rem(y + lax.rem(lax.div(k, 8), 4), 4),
            lax.rem(z + lax.rem(lax.div(k, 2), 4), 4),
            lax.rem(core + lax.rem(k, 2), 2),
        )

    def across(core2):
        return {"row": y, "col": col, "ch": (1 - low) * 2 + core2}

    mine = group(b, y, z, core)
    spot = y * 2 + core

    barrier = pltpu.get_barrier_semaphore()

    def greet(t, carry):
        pl.semaphore_signal(barrier, inc=1, device_id=place(*peer(t)), device_id_type=MESH)
        return carry

    for core2 in range(2):
        pl.semaphore_signal(barrier, inc=1, device_id=across(core2), device_id_type=MESH)
    lax.fori_loop(1, PEERS, greet, 0)
    pl.semaphore_wait(barrier, PEERS + 1)

    def send_pairs(r, carry):
        for step in range(1, 4):
            ch2 = lax.rem(ch + step, 4)
            quarter2 = lax.rem(lax.div(ch2, 2) + b, 2) * 2 + lax.rem(ch2, 2)
            rows = pl.ds(pl.multiple_of(quarter2 * tall + r * STEP, STEP), STEP)
            pltpu.make_async_remote_copy(
                src_ref=pair_ref.at[:, rows, :],
                dst_ref=pairs.at[pl.ds(ch * chan_part, chan_part), part_rows(r), :],
                send_sem=send_sem.at[0],
                recv_sem=pair_sem.at[r],
                device_id={"row": y, "col": col, "ch": ch2},
                device_id_type=MESH,
            ).start()
        rows = pl.ds(pl.multiple_of(quarter * tall + r * STEP, STEP), STEP)
        pltpu.make_async_copy(
            pair_ref.at[:, rows, :],
            pairs.at[pl.ds(ch * chan_part, chan_part), part_rows(r), :],
            own_pair_sem.at[r],
        ).start()
        return carry

    lax.fori_loop(0, PARTS, send_pairs, 0)

    chans = pairs.shape[0]
    hids = hidden.shape[0]

    def make_hidden(r, carry):
        held = pairs.at[pl.ds(0, 3 * chan_part), pl.ds(0, STEP), :]
        pltpu.make_async_copy(held, held, pair_sem.at[r]).wait()
        held = pairs.at[pl.ds(0, chan_part), pl.ds(0, STEP), :]
        pltpu.make_async_copy(held, held, own_pair_sem.at[r]).wait()
        flat[...] = pairs[:, part_rows(r), :].astype(jnp.float32).reshape(chans * STEP, LANES)
        mask = mask_ref[part_rows(r), :]
        for i in range(0, STEP, 2):
            both = [
                norm_rows(flat[pl.ds(i + d, chans, stride=STEP), :], gain_in_ref[...], bias_in_ref[...])
                for d in range(2)
            ]
            prod = jnp.dot(
                weight_in_ref[...], jnp.concatenate(both, axis=1), preferred_element_type=jnp.float32
            )
            for d in range(2):
                part = prod[:, d * LANES : (d + 1) * LANES]
                act = sigmoid(part[: 2 * hids]) * part[2 * hids : 4 * hids] * mask[i + d : i + d + 1, :]
                stage[pl.ds(i + d, 2 * hids, stride=STEP), :] = act
                gates[r * STEP + (i + d)] = sigmoid(part[4 * hids :])
        rounded = stage[...].astype(jnp.bfloat16).reshape(2, hids, STEP, LANES)
        hidden[:, 0, part_rows(r), :] = rounded[0]
        hidden[:, 1, part_rows(r), :] = rounded[1]
        here = pl.ds(pl.multiple_of(r * (8 * STEP) + spot * STEP, STEP), STEP)

        def send_acts(t, inner):
            to = peer(t)
            pltpu.make_async_remote_copy(
                src_ref=hidden.at[pl.ds(2 * group(*to), 2), :, part_rows(r), :],
                dst_ref=acts.at[:, :, col, here, :],
                send_sem=send_sem.at[1],
                recv_sem=act_sem.at[r],
                device_id=place(*to),
                device_id_type=MESH,
            ).start()
            return inner

        lax.fori_loop(1, PEERS, send_acts, 0)
        pltpu.make_async_copy(
            hidden.at[pl.ds(2 * mine, 2), :, part_rows(r), :], acts.at[:, :, col, here, :], own_act_sem.at[r]
        ).start()
        return carry

    lax.fori_loop(0, PARTS, make_hidden, 0)

    def pass_right(r, carry):
        held = hidden.at[pl.ds(0, 2 * PEERS - 2), :, pl.ds(0, STEP), :]
        pltpu.make_async_copy(held, held, act_sem.at[r]).wait()
        held = hidden.at[pl.ds(0, 2), :, pl.ds(0, STEP), :]
        pltpu.make_async_copy(held, held, own_act_sem.at[r]).wait()
        rows = pl.ds(pl.multiple_of(r * (8 * STEP), 8 * STEP), 8 * STEP)
        pltpu.make_async_remote_copy(
            src_ref=acts.at[:, 1, :, rows, :],
            dst_ref=far.at[:, :, rows, :],
            send_sem=send_sem.at[2],
            recv_sem=far_sem,
            device_id=across(core),
            device_id_type=MESH,
        ).start()
        return carry

    lax.fori_loop(0, PARTS, pass_right, 0)

    def multiply(turn, load_right):
        which = lax.rem(half + turn, 2)

        def block(n, carry):
            h, m = lax.div(n, 2), lax.rem(n, 2)
            left = jnp.concatenate([acts[h, 0, c] for c in range(8)], axis=1)
            right = []
            for c in range(8):
                right.append(
                    jnp.concatenate(
                        [
                            load_right(h, c, pl.ds(pl.multiple_of(m * (4 * STEP) + (r * 8 + s) * STEP, STEP), STEP))
                            for s2 in range(2)
                            for s in (s2 * 2, s2 * 2 + 1)
                            for r in range(PARTS)
                        ],
                        axis=0,
                    )
                )
            prod = lax.dot_general(
                left,
                jnp.concatenate(right, axis=1),
                (((1,), (1,)), ((), ())),
                preferred_element_type=jnp.float32,
            ).astype(jnp.bfloat16)
            for s in range(2):
                tri[h, (m * 2 + s) * 2 + which] = prod[:, s * LANES : (s + 1) * LANES].reshape(
                    PARTS, 8 * STEP, LANES
                )
            return carry

        lax.fori_loop(0, 4, block, 0)

        def send_round(n, carry):
            part = pl.ds(n * PER, PER)

            def send_sums(t, inner):
                k = lax.rem(t * 13, PEERS // 2)
                b2 = lax.rem(b + lax.div(k, 16), 2)
                y2 = lax.rem(y + lax.rem(lax.div(k, 4), 4), 4)
                z2 = 2 * lax.rem(lax.div(z, 2) + lax.rem(lax.div(k, 2), 2), 2) + which
                core2 = lax.rem(core + lax.rem(k, 2), 2)
                src = tri.at[
                    :, b2 * 4 + z2, part, pl.ds(pl.multiple_of((y2 * 2 + core2) * STEP, STEP), STEP), :
                ]
                dst = sums.at[pl.ds(2 * mine, 2), part]
                self = jnp.logical_and(t == 0, lax.rem(z, 2) == which)

                @pl.when(self)
                def _():
                    pltpu.make_async_copy(src, dst, own_sum_sem.at[n]).start()

                @pl.when(jnp.logical_not(self))
                def _():
                    pltpu.make_async_remote_copy(
                        src_ref=src,
                        dst_ref=dst,
                        send_sem=send_sem.at[3],
                        recv_sem=sum_sem.at[n],
                        device_id=place(b2, y2, z2, core2),
                        device_id_type=MESH,
                    ).start()

                return inner

            lax.fori_loop(0, PEERS // 2, send_sums, 0)
            return carry

        lax.fori_loop(0, ROUNDS, send_round, 0)

    multiply(0, lambda h, c, rows: acts[h, 1, c, rows, :])
    pltpu.make_async_copy(far, far, far_sem).wait()
    multiply(1, lambda h, c, rows: far[h, c, rows, :])

    def make_update(r, carry):
        flat[...] = sums[:, r].astype(jnp.float32).reshape(hids * STEP, LANES)
        for i in range(0, STEP, 2):
            both = [
                norm_rows(flat[pl.ds(i + d, hids, stride=STEP), :], gain_out_ref[...], bias_out_ref[...])
                for d in range(2)
            ]
            prod = jnp.dot(
                weight_out_ref[...], jnp.concatenate(both, axis=1), preferred_element_type=jnp.float32
            )
            for d in range(2):
                stage[pl.ds(i + d, chans, stride=STEP), :] = (
                    gates[r * STEP + (i + d)] * prod[:, d * LANES : (d + 1) * LANES]
                )
        result[:, part_rows(r), :] = (
            stage[pl.ds(0, chans * STEP), :].astype(jnp.bfloat16).reshape(chans, STEP, LANES)
        )
        rows = pl.ds(pl.multiple_of(quarter * tall + r * STEP, STEP), STEP)
        for step in range(1, 4):
            ch2 = lax.rem(ch + step, 4)
            pltpu.make_async_remote_copy(
                src_ref=result.at[pl.ds(ch2 * chan_part, chan_part), part_rows(r), :],
                dst_ref=out_ref.at[:, rows, :],
                send_sem=send_sem.at[4],
                recv_sem=out_sem,
                device_id={"row": y, "col": col, "ch": ch2},
                device_id_type=MESH,
            ).start()
        pltpu.make_async_copy(
            result.at[pl.ds(ch * chan_part, chan_part), part_rows(r), :], out_ref.at[:, rows, :], own_out_sem
        ).start()
        return carry

    def take_round(n, carry):
        held = sums.at[pl.ds(0, 2 * PEERS - 2), pl.ds(0, PER)]
        pltpu.make_async_copy(held, held, sum_sem.at[n]).wait()
        held = sums.at[pl.ds(0, 2), pl.ds(0, PER)]
        pltpu.make_async_copy(held, held, own_sum_sem.at[n]).wait()
        lax.fori_loop(n * PER, n * PER + PER, make_update, 0)
        return carry

    lax.fori_loop(0, ROUNDS, take_round, 0)

    held = result.at[pl.ds(0, 3 * chan_part)]
    pltpu.make_async_copy(held, held, out_sem).wait()
    held = result.at[pl.ds(0, chan_part)]
    pltpu.make_async_copy(held, held, own_out_sem).wait()
    for n, held in enumerate(
        (
            pairs.at[pl.ds(0, 3 * chan_part)],
            hidden.at[pl.ds(0, 2 * PEERS - 2)],
            far,
            sums.at[pl.ds(0, 2 * PEERS - 2)],
            result.at[pl.ds(0, 3 * chan_part)],
        )
    ):
        pltpu.make_async_copy(held, held, send_sem.at[n]).wait()


def local(pair, token_mask, gain_in, bias_in, proj_in, gate_in, gain_out, bias_out, proj_out, gate_out):
    chan_part, row_count, lanes = pair.shape
    chs = lax.axis_size("ch")
    chans, hids = chan_part * chs, proj_out.shape[0]
    tall = row_count // chs
    ch, col = lax.axis_index("ch"), lax.axis_index("col")
    quarter = (ch // 2 + col // 4) % 2 * 2 + ch % 2
    row_start = lax.axis_index("row") * row_count + quarter * tall
    row_mask = lax.dynamic_slice_in_dim(token_mask, row_start, tall, 0).astype(jnp.float32)
    col_mask = lax.dynamic_slice_in_dim(token_mask, col * lanes, lanes, 0).astype(jnp.float32)
    mask = row_mask[:, None] * col_mask[None, :]
    wide = lambda v: jnp.broadcast_to(v[:, None], (v.shape[0], lanes))
    weight = jnp.concatenate([gate_in, proj_in, gate_out], axis=1).T
    vmem = pl.BlockSpec(memory_space=pltpu.VMEM)
    half16 = lambda *shape: pltpu.VMEM(shape, jnp.bfloat16)
    dma = pltpu.SemaphoreType.DMA
    return pl.pallas_call(
        kernel,
        name="update",
        out_shape=jax.ShapeDtypeStruct(pair.shape, jnp.bfloat16),
        in_specs=[pl.BlockSpec(memory_space=pl.ANY)] + [vmem] * 7,
        out_specs=pl.BlockSpec(memory_space=pl.ANY),
        scratch_shapes=[
            half16(chans, tall, lanes),
            half16(hids, 2, tall, lanes),
            pltpu.VMEM((tall, chans, lanes), jnp.float32),
            half16(2, 2, 8, PARTS * 8 * STEP, lanes),
            half16(2, 8, PARTS * 8 * STEP, lanes),
            half16(2, 8, PARTS, 8 * STEP, lanes),
            half16(hids, PARTS, STEP, lanes),
            half16(chans, tall, lanes),
            pltpu.VMEM((chans * STEP, lanes), jnp.float32),
            pltpu.VMEM((2 * hids * STEP, lanes), jnp.float32),
            dma((5,)),
            dma((PARTS,)),
            dma((PARTS,)),
            dma,
            dma((ROUNDS,)),
            dma,
            dma((PARTS,)),
            dma((PARTS,)),
            dma((ROUNDS,)),
            dma,
        ],
        compiler_params=pltpu.CompilerParams(
            collective_id=0, has_side_effects=True, vmem_limit_bytes=56 * 2**20
        ),
    )(pair, mask, wide(gain_in), wide(bias_in), weight, wide(gain_out), wide(bias_out), proj_out.T)


def solution(mesh):
    in_specs = (P("ch", "row", "col"),) + (P(),) * 9
    return jax.shard_map(local, mesh=mesh, in_specs=in_specs, out_specs=P("ch", "row", "col"), check_vma=False)
```

```python
import functools

import jax
import jax.numpy as jnp
from jax import lax
from jax.experimental import pallas as pl
from jax.experimental.pallas import tpu as pltpu
from jax.sharding import PartitionSpec as P

epsilon = 1e-05
MESH = pl.DeviceIdType.MESH
STEP = 16
PARTS = 4
ROUNDS = 4
PER = PARTS // ROUNDS
LANES = 128
PEERS = 64


def norm_rows(values, gain, bias):
    width = values.shape[0]
    center = jnp.sum(values, axis=0, keepdims=True) * (1.0 / width)
    second = jnp.sum(values * values, axis=0, keepdims=True) * (1.0 / width)
    spread = second - center * center
    return ((values - center) * lax.rsqrt(spread + epsilon) * gain + bias).astype(jnp.bfloat16)


def sigmoid(values):
    return 0.5 * jnp.tanh(0.5 * values) + 0.5


def part_rows(r):
    return pl.ds(pl.multiple_of(r * STEP, STEP), STEP)


def kernel(
    pair_ref,
    token_ref,
    gain_in_ref,
    bias_in_ref,
    proj_in_ref,
    gate_in_ref,
    gain_out_ref,
    bias_out_ref,
    proj_out_ref,
    gate_out_ref,
    out_ref,
    pairs,
    hidden,
    gates,
    acts,
    far,
    tri,
    sums,
    result,
    flat,
    stage,
    mask,
    affine,
    weight_in,
    weight_out,
    send_sem,
    pair_sem,
    act_sem,
    far_sem,
    sum_sem,
    out_sem,
    own_pair_sem,
    own_act_sem,
    own_sum_sem,
    own_out_sem,
):
    y, col, ch = lax.axis_index("row"), lax.axis_index("col"), lax.axis_index("ch")
    b, z = lax.div(col, 4), lax.rem(col, 4)
    low, core = lax.div(ch, 2), lax.rem(ch, 2)
    half = lax.rem(low + b, 2)
    quarter = half * 2 + core
    chan_part = pair_ref.shape[0]
    tall = STEP * PARTS

    def place(b2, y2, z2, core2):
        return {"row": y2, "col": b2 * 4 + z2, "ch": lax.rem(half + b2, 2) * 2 + core2}

    def group(b2, y2, z2, core2):
        return ((b2 * 4 + y2) * 4 + z2) * 2 + core2

    def peer(t):
        k = lax.rem(t * 37, PEERS)
        return (
            lax.rem(b + lax.div(k, 32), 2),
            lax.rem(y + lax.rem(lax.div(k, 8), 4), 4),
            lax.rem(z + lax.rem(lax.div(k, 2), 4), 4),
            lax.rem(core + lax.rem(k, 2), 2),
        )

    def across(core2):
        return {"row": y, "col": col, "ch": (1 - low) * 2 + core2}

    mine = group(b, y, z, core)
    spot = y * 2 + core

    barrier = pltpu.get_barrier_semaphore()

    def greet(t, carry):
        pl.semaphore_signal(barrier, inc=1, device_id=place(*peer(t)), device_id_type=MESH)
        return carry

    for core2 in range(2):
        pl.semaphore_signal(barrier, inc=1, device_id=across(core2), device_id_type=MESH)
    lax.fori_loop(1, PEERS, greet, 0)
    pl.semaphore_wait(barrier, PEERS + 1)

    def send_pairs(r, carry):
        for step in range(1, 4):
            ch2 = lax.rem(ch + step, 4)
            quarter2 = lax.rem(lax.div(ch2, 2) + b, 2) * 2 + lax.rem(ch2, 2)
            rows = pl.ds(pl.multiple_of(quarter2 * tall + r * STEP, STEP), STEP)
            pltpu.make_async_remote_copy(
                src_ref=pair_ref.at[:, rows, :],
                dst_ref=pairs.at[pl.ds(ch * chan_part, chan_part), part_rows(r), :],
                send_sem=send_sem.at[0],
                recv_sem=pair_sem.at[r],
                device_id={"row": y, "col": col, "ch": ch2},
                device_id_type=MESH,
            ).start()
        rows = pl.ds(pl.multiple_of(quarter * tall + r * STEP, STEP), STEP)
        pltpu.make_async_copy(
            pair_ref.at[:, rows, :],
            pairs.at[pl.ds(ch * chan_part, chan_part), part_rows(r), :],
            own_pair_sem.at[r],
        ).start()
        return carry

    lax.fori_loop(0, PARTS, send_pairs, 0)

    chans = pairs.shape[0]
    hids = hidden.shape[0]

    def turned(ref):
        return ref[...].astype(jnp.float32).T.astype(jnp.bfloat16)

    def column(vec):
        return jnp.broadcast_to(vec, (LANES, LANES)).T

    weight_in[: 2 * hids] = turned(gate_in_ref)
    weight_in[2 * hids : 4 * hids] = turned(proj_in_ref)
    weight_in[4 * hids :] = turned(gate_out_ref)
    weight_out[...] = turned(proj_out_ref)
    for n, ref in enumerate((gain_in_ref, bias_in_ref, gain_out_ref, bias_out_ref)):
        affine[n] = column(ref[...])
    mask[...] = column(token_ref[pl.ds(y * 2 + half, 1), :].astype(jnp.float32)) * token_ref[
        pl.ds(col, 1), :
    ].astype(jnp.float32)

    def make_hidden(r, carry):
        held = pairs.at[pl.ds(0, 3 * chan_part), pl.ds(0, STEP), :]
        pltpu.make_async_copy(held, held, pair_sem.at[r]).wait()
        held = pairs.at[pl.ds(0, chan_part), pl.ds(0, STEP), :]
        pltpu.make_async_copy(held, held, own_pair_sem.at[r]).wait()
        flat[...] = pairs[:, part_rows(r), :].astype(jnp.float32).reshape(chans * STEP, LANES)
        here_mask = mask[pl.ds(pl.multiple_of(core * tall + r * STEP, STEP), STEP), :]
        for i in range(0, STEP, 2):
            both = [
                norm_rows(flat[pl.ds(i + d, chans, stride=STEP), :], affine[0], affine[1])
                for d in range(2)
            ]
            prod = jnp.dot(
                weight_in[...], jnp.concatenate(both, axis=1), preferred_element_type=jnp.float32
            )
            for d in range(2):
                part = prod[:, d * LANES : (d + 1) * LANES]
                act = sigmoid(part[: 2 * hids]) * part[2 * hids : 4 * hids] * here_mask[i + d : i + d + 1, :]
                stage[pl.ds(i + d, 2 * hids, stride=STEP), :] = act
                gates[r * STEP + (i + d)] = sigmoid(part[4 * hids :])
        rounded = stage[...].astype(jnp.bfloat16).reshape(2, hids, STEP, LANES)
        hidden[:, 0, part_rows(r), :] = rounded[0]
        hidden[:, 1, part_rows(r), :] = rounded[1]
        here = pl.ds(pl.multiple_of(r * (8 * STEP) + spot * STEP, STEP), STEP)

        def send_acts(t, inner):
            to = peer(t)
            pltpu.make_async_remote_copy(
                src_ref=hidden.at[pl.ds(2 * group(*to), 2), :, part_rows(r), :],
                dst_ref=acts.at[:, :, col, here, :],
                send_sem=send_sem.at[1],
                recv_sem=act_sem.at[r],
                device_id=place(*to),
                device_id_type=MESH,
            ).start()
            return inner

        lax.fori_loop(1, PEERS, send_acts, 0)
        pltpu.make_async_copy(
            hidden.at[pl.ds(2 * mine, 2), :, part_rows(r), :], acts.at[:, :, col, here, :], own_act_sem.at[r]
        ).start()
        return carry

    lax.fori_loop(0, PARTS, make_hidden, 0)

    def pass_right(r, carry):
        held = hidden.at[pl.ds(0, 2 * PEERS - 2), :, pl.ds(0, STEP), :]
        pltpu.make_async_copy(held, held, act_sem.at[r]).wait()
        held = hidden.at[pl.ds(0, 2), :, pl.ds(0, STEP), :]
        pltpu.make_async_copy(held, held, own_act_sem.at[r]).wait()
        rows = pl.ds(pl.multiple_of(r * (8 * STEP), 8 * STEP), 8 * STEP)
        pltpu.make_async_remote_copy(
            src_ref=acts.at[:, 1, :, rows, :],
            dst_ref=far.at[:, :, rows, :],
            send_sem=send_sem.at[2],
            recv_sem=far_sem,
            device_id=across(core),
            device_id_type=MESH,
        ).start()
        return carry

    lax.fori_loop(0, PARTS, pass_right, 0)

    def multiply(turn, load_right):
        which = lax.rem(half + turn, 2)

        def block(n, carry):
            h, m = lax.div(n, 2), lax.rem(n, 2)
            left = jnp.concatenate([acts[h, 0, c] for c in range(8)], axis=1)
            right = []
            for c in range(8):
                right.append(
                    jnp.concatenate(
                        [
                            load_right(h, c, pl.ds(pl.multiple_of(m * (4 * STEP) + (r * 8 + s) * STEP, STEP), STEP))
                            for s2 in range(2)
                            for s in (s2 * 2, s2 * 2 + 1)
                            for r in range(PARTS)
                        ],
                        axis=0,
                    )
                )
            prod = lax.dot_general(
                left,
                jnp.concatenate(right, axis=1),
                (((1,), (1,)), ((), ())),
                preferred_element_type=jnp.float32,
            ).astype(jnp.bfloat16)
            for s in range(2):
                tri[h, (m * 2 + s) * 2 + which] = prod[:, s * LANES : (s + 1) * LANES].reshape(
                    PARTS, 8 * STEP, LANES
                )
            return carry

        lax.fori_loop(0, 4, block, 0)

    multiply(0, lambda h, c, rows: acts[h, 1, c, rows, :])
    pltpu.make_async_copy(far, far, far_sem).wait()
    multiply(1, lambda h, c, rows: far[h, c, rows, :])

    def send_round(n, carry):
        part = pl.ds(n * PER, PER)

        def send_sums(t, inner):
            b2, y2, z2, core2 = peer(t)
            pltpu.make_async_remote_copy(
                src_ref=tri.at[
                    :, b2 * 4 + z2, part, pl.ds(pl.multiple_of((y2 * 2 + core2) * STEP, STEP), STEP), :
                ],
                dst_ref=sums.at[pl.ds(2 * mine, 2), part],
                send_sem=send_sem.at[3],
                recv_sem=sum_sem.at[n],
                device_id=place(b2, y2, z2, core2),
                device_id_type=MESH,
            ).start()
            return inner

        lax.fori_loop(1, PEERS, send_sums, 0)
        pltpu.make_async_copy(
            tri.at[:, col, part, pl.ds(pl.multiple_of(spot * STEP, STEP), STEP), :],
            sums.at[pl.ds(2 * mine, 2), part],
            own_sum_sem.at[n],
        ).start()
        return carry

    lax.fori_loop(0, ROUNDS, send_round, 0)

    def make_update(r, carry):
        flat[...] = sums[:, r].astype(jnp.float32).reshape(hids * STEP, LANES)
        for i in range(0, STEP, 2):
            both = [
                norm_rows(flat[pl.ds(i + d, hids, stride=STEP), :], affine[2], affine[3])
                for d in range(2)
            ]
            prod = jnp.dot(
                weight_out[...], jnp.concatenate(both, axis=1), preferred_element_type=jnp.float32
            )
            for d in range(2):
                stage[pl.ds(i + d, chans, stride=STEP), :] = (
                    gates[r * STEP + (i + d)] * prod[:, d * LANES : (d + 1) * LANES]
                )
        result[:, part_rows(r), :] = (
            stage[pl.ds(0, chans * STEP), :].astype(jnp.bfloat16).reshape(chans, STEP, LANES)
        )
        rows = pl.ds(pl.multiple_of(quarter * tall + r * STEP, STEP), STEP)
        for step in range(1, 4):
            ch2 = lax.rem(ch + step, 4)
            pltpu.make_async_remote_copy(
                src_ref=result.at[pl.ds(ch2 * chan_part, chan_part), part_rows(r), :],
                dst_ref=out_ref.at[:, rows, :],
                send_sem=send_sem.at[4],
                recv_sem=out_sem,
                device_id={"row": y, "col": col, "ch": ch2},
                device_id_type=MESH,
            ).start()
        pltpu.make_async_copy(
            result.at[pl.ds(ch * chan_part, chan_part), part_rows(r), :], out_ref.at[:, rows, :], own_out_sem
        ).start()
        return carry

    def take_round(n, carry):
        held = sums.at[pl.ds(0, 2 * PEERS - 2), pl.ds(0, PER)]
        pltpu.make_async_copy(held, held, sum_sem.at[n]).wait()
        held = sums.at[pl.ds(0, 2), pl.ds(0, PER)]
        pltpu.make_async_copy(held, held, own_sum_sem.at[n]).wait()
        lax.fori_loop(n * PER, n * PER + PER, make_update, 0)
        return carry

    lax.fori_loop(0, ROUNDS, take_round, 0)

    held = result.at[pl.ds(0, 3 * chan_part)]
    pltpu.make_async_copy(held, held, out_sem).wait()
    held = result.at[pl.ds(0, chan_part)]
    pltpu.make_async_copy(held, held, own_out_sem).wait()
    for n, held in enumerate(
        (
            pairs.at[pl.ds(0, 3 * chan_part)],
            hidden.at[pl.ds(0, 2 * PEERS - 2)],
            far,
            sums.at[pl.ds(0, 2 * PEERS - 2)],
            result.at[pl.ds(0, 3 * chan_part)],
        )
    ):
        pltpu.make_async_copy(held, held, send_sem.at[n]).wait()


def local(pair, token_mask, gain_in, bias_in, proj_in, gate_in, gain_out, bias_out, proj_out, gate_out):
    chan_part, row_count, lanes = pair.shape
    chs = lax.axis_size("ch")
    chans, hids = chan_part * chs, proj_out.shape[0]
    tall = row_count // chs
    vmem = pl.BlockSpec(memory_space=pltpu.VMEM)
    half16 = lambda *shape: pltpu.VMEM(shape, jnp.bfloat16)
    dma = pltpu.SemaphoreType.DMA
    return pl.pallas_call(
        kernel,
        name="update",
        out_shape=jax.ShapeDtypeStruct(pair.shape, jnp.bfloat16),
        in_specs=[pl.BlockSpec(memory_space=pl.ANY)] + [vmem] * 9,
        out_specs=pl.BlockSpec(memory_space=pl.ANY),
        scratch_shapes=[
            half16(chans, tall, lanes),
            half16(hids, 2, tall, lanes),
            pltpu.VMEM((tall, chans, lanes), jnp.float32),
            half16(2, 2, 8, PARTS * 8 * STEP, lanes),
            half16(2, 8, PARTS * 8 * STEP, lanes),
            half16(2, 8, PARTS, 8 * STEP, lanes),
            half16(hids, PARTS, STEP, lanes),
            half16(chans, tall, lanes),
            pltpu.VMEM((chans * STEP, lanes), jnp.float32),
            pltpu.VMEM((2 * hids * STEP, lanes), jnp.float32),
            pltpu.VMEM((lanes, lanes), jnp.float32),
            pltpu.VMEM((4, lanes, lanes), jnp.float32),
            half16(4 * hids + chans, chans),
            half16(chans, hids),
            dma((5,)),
            dma((PARTS,)),
            dma((PARTS,)),
            dma,
            dma((ROUNDS,)),
            dma,
            dma((PARTS,)),
            dma((PARTS,)),
            dma((ROUNDS,)),
            dma,
        ],
        compiler_params=pltpu.CompilerParams(
            collective_id=0, has_side_effects=True, vmem_limit_bytes=56 * 2**20
        ),
    )(
        pair,
        token_mask.reshape(-1, lanes),
        gain_in.reshape(1, -1),
        bias_in.reshape(1, -1),
        proj_in,
        gate_in,
        gain_out.reshape(1, -1),
        bias_out.reshape(1, -1),
        proj_out,
        gate_out,
    )


def solution(mesh):
    in_specs = (P("ch", "row", "col"),) + (P(),) * 9
    return jax.shard_map(local, mesh=mesh, in_specs=in_specs, out_specs=P("ch", "row", "col"), check_vma=False)
```

```python
import functools

import jax
import jax.numpy as jnp
from jax import lax
from jax.experimental import pallas as pl
from jax.experimental.pallas import tpu as pltpu
from jax.sharding import PartitionSpec as P

epsilon = 1e-05
MESH = pl.DeviceIdType.MESH
STEP = 16
PARTS = 4
ROUNDS = 4
PER = PARTS // ROUNDS
LANES = 128
SPARE = PARTS - 1
PEERS = 64


def norm_rows(values, gain, bias):
    width = values.shape[0]
    center = jnp.sum(values, axis=0, keepdims=True) * (1.0 / width)
    second = jnp.sum(values * values, axis=0, keepdims=True) * (1.0 / width)
    spread = second - center * center
    return ((values - center) * lax.rsqrt(spread + epsilon) * gain + bias).astype(jnp.bfloat16)


def sigmoid(values):
    return 0.5 * jnp.tanh(0.5 * values) + 0.5


def part_rows(r):
    return pl.ds(pl.multiple_of(r * STEP, STEP), STEP)


def kernel(
    pair_ref,
    token_hbm,
    gain_in_hbm,
    bias_in_hbm,
    proj_in_hbm,
    gate_in_hbm,
    gain_out_hbm,
    bias_out_hbm,
    proj_out_hbm,
    gate_out_hbm,
    out_ref,
    pairs,
    hidden,
    gates,
    acts,
    far,
    tri,
    sums,
    result,
    flat,
    stage,
    mask,
    affine,
    weight_in,
    weight_out,
    extra,
    token_ref,
    gain_in_ref,
    bias_in_ref,
    proj_in_ref,
    gate_in_ref,
    gain_out_ref,
    bias_out_ref,
    proj_out_ref,
    gate_out_ref,
    send_sem,
    pair_sem,
    act_sem,
    extra_sem,
    far_sem,
    sum_sem,
    out_sem,
    own_pair_sem,
    own_act_sem,
    own_extra_sem,
    own_sum_sem,
    own_out_sem,
    small_sem,
):
    y, col, ch = lax.axis_index("row"), lax.axis_index("col"), lax.axis_index("ch")
    b, z = lax.div(col, 4), lax.rem(col, 4)
    low, core = lax.div(ch, 2), lax.rem(ch, 2)
    half = lax.rem(low + b, 2)
    quarter = half * 2 + core
    chan_part = pair_ref.shape[0]
    tall = STEP * PARTS

    def place(b2, y2, z2, core2):
        return {"row": y2, "col": b2 * 4 + z2, "ch": lax.rem(half + b2, 2) * 2 + core2}

    def group(b2, y2, z2, core2):
        return ((b2 * 4 + y2) * 4 + z2) * 2 + core2

    def peer(t):
        k = lax.rem(t * 37, PEERS)
        return (
            lax.rem(b + lax.div(k, 32), 2),
            lax.rem(y + lax.rem(lax.div(k, 8), 4), 4),
            lax.rem(z + lax.rem(lax.div(k, 2), 4), 4),
            lax.rem(core + lax.rem(k, 2), 2),
        )

    def across(core2):
        return {"row": y, "col": col, "ch": (1 - low) * 2 + core2}

    small = [
        pltpu.make_async_copy(src, dst, small_sem.at[n])
        for n, (src, dst) in enumerate(
            (
                (token_hbm, token_ref),
                (gain_in_hbm, gain_in_ref),
                (bias_in_hbm, bias_in_ref),
                (proj_in_hbm, proj_in_ref),
                (gate_in_hbm, gate_in_ref),
                (gain_out_hbm, gain_out_ref),
                (bias_out_hbm, bias_out_ref),
                (proj_out_hbm, proj_out_ref),
                (gate_out_hbm, gate_out_ref),
            )
        )
    ]
    for copy in small:
        copy.start()

    mine = group(b, y, z, core)
    spot = y * 2 + core

    barrier = pltpu.get_barrier_semaphore()

    def greet(t, carry):
        pl.semaphore_signal(barrier, inc=1, device_id=place(*peer(t)), device_id_type=MESH)
        return carry

    for core2 in range(2):
        pl.semaphore_signal(barrier, inc=1, device_id=across(core2), device_id_type=MESH)
    lax.fori_loop(1, PEERS, greet, 0)
    pl.semaphore_wait(barrier, PEERS + 1)

    def rows_for(half2, core2, r):
        spare = lax.div(r, PARTS)
        half2 = lax.rem(half2 + spare, 2)
        return pl.ds(pl.multiple_of((half2 * 2 + core2) * tall + (r - spare) * STEP, STEP), STEP)

    def send_pairs(r, carry):
        for step in range(1, 4):
            ch2 = lax.rem(ch + step, 4)
            pltpu.make_async_remote_copy(
                src_ref=pair_ref.at[:, rows_for(lax.rem(lax.div(ch2, 2) + b, 2), lax.rem(ch2, 2), r), :],
                dst_ref=pairs.at[pl.ds(ch * chan_part, chan_part), part_rows(r), :],
                send_sem=send_sem.at[0],
                recv_sem=pair_sem.at[r],
                device_id={"row": y, "col": col, "ch": ch2},
                device_id_type=MESH,
            ).start()
        pltpu.make_async_copy(
            pair_ref.at[:, rows_for(half, core, r), :],
            pairs.at[pl.ds(ch * chan_part, chan_part), part_rows(r), :],
            own_pair_sem.at[r],
        ).start()
        return carry

    lax.fori_loop(0, PARTS + 1, send_pairs, 0)

    chans = pairs.shape[0]
    hids = hidden.shape[0]

    def turned(ref):
        return ref[...].astype(jnp.float32).T.astype(jnp.bfloat16)

    def column(vec):
        return jnp.broadcast_to(vec, (LANES, LANES)).T

    for copy in small:
        copy.wait()
    weight_in[: 2 * hids] = turned(gate_in_ref)
    weight_in[2 * hids : 4 * hids] = turned(proj_in_ref)
    weight_in[4 * hids :] = turned(gate_out_ref)
    weight_out[...] = turned(proj_out_ref)
    for n, ref in enumerate((gain_in_ref, bias_in_ref, gain_out_ref, bias_out_ref)):
        affine[n] = column(ref[...])
    for n in range(2):
        mask[n] = column(
            token_ref[pl.ds(y * 2 + lax.rem(half + n, 2), 1), :].astype(jnp.float32)
        ) * token_ref[pl.ds(col, 1), :].astype(jnp.float32)

    def take_pairs(r):
        held = pairs.at[pl.ds(0, 3 * chan_part), pl.ds(0, STEP), :]
        pltpu.make_async_copy(held, held, pair_sem.at[r]).wait()
        held = pairs.at[pl.ds(0, chan_part), pl.ds(0, STEP), :]
        pltpu.make_async_copy(held, held, own_pair_sem.at[r]).wait()
        flat[...] = pairs[:, part_rows(r), :].astype(jnp.float32).reshape(chans * STEP, LANES)

    def normed(i):
        both = [
            norm_rows(flat[pl.ds(i + d, chans, stride=STEP), :], affine[0], affine[1]) for d in range(2)
        ]
        return jnp.concatenate(both, axis=1)

    def make_hidden(r, carry):
        take_pairs(r)
        here_mask = mask[0, pl.ds(pl.multiple_of(core * tall + r * STEP, STEP), STEP), :]
        for i in range(0, STEP, 2):
            prod = jnp.dot(weight_in[...], normed(i), preferred_element_type=jnp.float32)
            for d in range(2):
                part = prod[:, d * LANES : (d + 1) * LANES]
                act = sigmoid(part[: 2 * hids]) * part[2 * hids : 4 * hids] * here_mask[i + d : i + d + 1, :]
                stage[pl.ds(i + d, 2 * hids, stride=STEP), :] = act
                gates[r * STEP + (i + d)] = sigmoid(part[4 * hids :])
        rounded = stage[...].astype(jnp.bfloat16).reshape(2, hids, STEP, LANES)
        hidden[:, 0, part_rows(r), :] = rounded[0]
        hidden[:, 1, part_rows(r), :] = rounded[1]
        here = pl.ds(pl.multiple_of(r * (8 * STEP) + spot * STEP, STEP), STEP)

        def send_acts(t, inner):
            to = peer(t)
            pltpu.make_async_remote_copy(
                src_ref=hidden.at[pl.ds(2 * group(*to), 2), :, part_rows(r), :],
                dst_ref=acts.at[:, :, col, here, :],
                send_sem=send_sem.at[1],
                recv_sem=act_sem.at[r],
                device_id=place(*to),
                device_id_type=MESH,
            ).start()
            return inner

        lax.fori_loop(1, PEERS, send_acts, 0)
        pltpu.make_async_copy(
            hidden.at[pl.ds(2 * mine, 2), :, part_rows(r), :], acts.at[:, :, col, here, :], own_act_sem.at[r]
        ).start()
        return carry

    lax.fori_loop(0, PARTS, make_hidden, 0)

    def take_acts(r):
        held = hidden.at[pl.ds(0, 2 * PEERS - 2), :, pl.ds(0, STEP), :]
        pltpu.make_async_copy(held, held, act_sem.at[r]).wait()
        held = hidden.at[pl.ds(0, 2), :, pl.ds(0, STEP), :]
        pltpu.make_async_copy(held, held, own_act_sem.at[r]).wait()

    def pass_right(r):
        take_acts(r)
        rows = pl.ds(r * (8 * STEP), 8 * STEP)
        pltpu.make_async_remote_copy(
            src_ref=acts.at[:, 1, :, rows, :],
            dst_ref=far.at[:, :, rows, :],
            send_sem=send_sem.at[2],
            recv_sem=far_sem,
            device_id=across(core),
            device_id_type=MESH,
        ).start()

    pass_right(0)

    take_pairs(PARTS)
    spare_mask = mask[1, pl.ds(pl.multiple_of(core * tall + SPARE * STEP, STEP), STEP), :]
    for i in range(0, STEP, 2):
        both = normed(i)
        gate = jnp.dot(weight_in[hids : 2 * hids], both, preferred_element_type=jnp.float32)
        prod = jnp.dot(weight_in[3 * hids : 4 * hids], both, preferred_element_type=jnp.float32)
        for d in range(2):
            lanes = slice(d * LANES, (d + 1) * LANES)
            stage[pl.ds(i + d, hids, stride=STEP), :] = (
                sigmoid(gate[:, lanes]) * prod[:, lanes] * spare_mask[i + d : i + d + 1, :]
            )
    extra[...] = stage[pl.ds(0, hids * STEP), :].astype(jnp.bfloat16).reshape(hids, STEP, LANES)
    spare_rows = pl.ds(pl.multiple_of(SPARE * (8 * STEP) + spot * STEP, STEP), STEP)

    def send_extra(t, carry):
        to = peer(t)
        pltpu.make_async_remote_copy(
            src_ref=extra.at[pl.ds(2 * group(*to), 2)],
            dst_ref=far.at[:, col, spare_rows, :],
            send_sem=send_sem.at[5],
            recv_sem=extra_sem,
            device_id=place(*to),
            device_id_type=MESH,
        ).start()
        return carry

    lax.fori_loop(1, PEERS, send_extra, 0)
    pltpu.make_async_copy(
        extra.at[pl.ds(2 * mine, 2)], far.at[:, col, spare_rows, :], own_extra_sem
    ).start()

    for r in range(1, SPARE):
        pass_right(r)
    take_acts(SPARE)

    def multiply(turn, load_right):
        which = lax.rem(half + turn, 2)

        def block(n, carry):
            h, m = lax.div(n, 2), lax.rem(n, 2)
            left = jnp.concatenate([acts[h, 0, c] for c in range(8)], axis=1)
            right = []
            for c in range(8):
                right.append(
                    jnp.concatenate(
                        [
                            load_right(h, c, pl.ds(pl.multiple_of(m * (4 * STEP) + (r * 8 + s) * STEP, STEP), STEP))
                            for s2 in range(2)
                            for s in (s2 * 2, s2 * 2 + 1)
                            for r in range(PARTS)
                        ],
                        axis=0,
                    )
                )
            prod = lax.dot_general(
                left,
                jnp.concatenate(right, axis=1),
                (((1,), (1,)), ((), ())),
                preferred_element_type=jnp.float32,
            ).astype(jnp.bfloat16)
            for s in range(2):
                tri[h, (m * 2 + s) * 2 + which] = prod[:, s * LANES : (s + 1) * LANES].reshape(
                    PARTS, 8 * STEP, LANES
                )
            return carry

        lax.fori_loop(0, 4, block, 0)

    multiply(0, lambda h, c, rows: acts[h, 1, c, rows, :])
    held = extra.at[pl.ds(0, 2 * PEERS - 2)]
    pltpu.make_async_copy(held, held, extra_sem).wait()
    held = extra.at[pl.ds(0, 2)]
    pltpu.make_async_copy(held, held, own_extra_sem).wait()
    held = far.at[:, :, pl.ds(0, SPARE * 8 * STEP), :]
    pltpu.make_async_copy(held, held, far_sem).wait()
    multiply(1, lambda h, c, rows: far[h, c, rows, :])

    def send_round(n, carry):
        part = pl.ds(n * PER, PER)

        def send_sums(t, inner):
            b2, y2, z2, core2 = peer(t)
            pltpu.make_async_remote_copy(
                src_ref=tri.at[
                    :, b2 * 4 + z2, part, pl.ds(pl.multiple_of((y2 * 2 + core2) * STEP, STEP), STEP), :
                ],
                dst_ref=sums.at[pl.ds(2 * mine, 2), part],
                send_sem=send_sem.at[3],
                recv_sem=sum_sem.at[n],
                device_id=place(b2, y2, z2, core2),
                device_id_type=MESH,
            ).start()
            return inner

        lax.fori_loop(1, PEERS, send_sums, 0)
        pltpu.make_async_copy(
            tri.at[:, col, part, pl.ds(pl.multiple_of(spot * STEP, STEP), STEP), :],
            sums.at[pl.ds(2 * mine, 2), part],
            own_sum_sem.at[n],
        ).start()
        return carry

    lax.fori_loop(0, ROUNDS, send_round, 0)

    def make_update(r, carry):
        flat[...] = sums[:, r].astype(jnp.float32).reshape(hids * STEP, LANES)
        for i in range(0, STEP, 2):
            both = [
                norm_rows(flat[pl.ds(i + d, hids, stride=STEP), :], affine[2], affine[3])
                for d in range(2)
            ]
            prod = jnp.dot(
                weight_out[...], jnp.concatenate(both, axis=1), preferred_element_type=jnp.float32
            )
            for d in range(2):
                stage[pl.ds(i + d, chans, stride=STEP), :] = (
                    gates[r * STEP + (i + d)] * prod[:, d * LANES : (d + 1) * LANES]
                )
        result[:, part_rows(r), :] = (
            stage[pl.ds(0, chans * STEP), :].astype(jnp.bfloat16).reshape(chans, STEP, LANES)
        )
        rows = pl.ds(pl.multiple_of(quarter * tall + r * STEP, STEP), STEP)
        for step in range(1, 4):
            ch2 = lax.rem(ch + step, 4)
            pltpu.make_async_remote_copy(
                src_ref=result.at[pl.ds(ch2 * chan_part, chan_part), part_rows(r), :],
                dst_ref=out_ref.at[:, rows, :],
                send_sem=send_sem.at[4],
                recv_sem=out_sem,
                device_id={"row": y, "col": col, "ch": ch2},
                device_id_type=MESH,
            ).start()
        pltpu.make_async_copy(
            result.at[pl.ds(ch * chan_part, chan_part), part_rows(r), :], out_ref.at[:, rows, :], own_out_sem
        ).start()
        return carry

    def take_round(n, carry):
        held = sums.at[pl.ds(0, 2 * PEERS - 2), pl.ds(0, PER)]
        pltpu.make_async_copy(held, held, sum_sem.at[n]).wait()
        held = sums.at[pl.ds(0, 2), pl.ds(0, PER)]
        pltpu.make_async_copy(held, held, own_sum_sem.at[n]).wait()
        lax.fori_loop(n * PER, n * PER + PER, make_update, 0)
        return carry

    lax.fori_loop(0, ROUNDS, take_round, 0)

    held = result.at[pl.ds(0, 3 * chan_part)]
    pltpu.make_async_copy(held, held, out_sem).wait()
    held = result.at[pl.ds(0, chan_part)]
    pltpu.make_async_copy(held, held, own_out_sem).wait()
    for n, held in enumerate(
        (
            pairs.at[pl.ds(0, 3 * chan_part)],
            hidden.at[pl.ds(0, 2 * PEERS - 2)],
            far.at[:, :, pl.ds(0, SPARE * 8 * STEP), :],
            sums.at[pl.ds(0, 2 * PEERS - 2)],
            result.at[pl.ds(0, 3 * chan_part)],
            extra.at[pl.ds(0, 2 * PEERS - 2)],
        )
    ):
        pltpu.make_async_copy(held, held, send_sem.at[n]).wait()


def local(pair, token_mask, gain_in, bias_in, proj_in, gate_in, gain_out, bias_out, proj_out, gate_out):
    chan_part, row_count, lanes = pair.shape
    chs = lax.axis_size("ch")
    chans, hids = chan_part * chs, proj_out.shape[0]
    tall = row_count // chs
    half16 = lambda *shape: pltpu.VMEM(shape, jnp.bfloat16)
    dma = pltpu.SemaphoreType.DMA
    return pl.pallas_call(
        kernel,
        name="update",
        out_shape=jax.ShapeDtypeStruct(pair.shape, jnp.bfloat16),
        in_specs=[pl.BlockSpec(memory_space=pl.ANY)] + [pl.BlockSpec(memory_space=pl.ANY)] * 9,
        out_specs=pl.BlockSpec(memory_space=pl.ANY),
        scratch_shapes=[
            half16(chans, tall + STEP, lanes),
            half16(hids, 2, tall, lanes),
            pltpu.VMEM((tall, chans, lanes), jnp.float32),
            half16(2, 2, 8, PARTS * 8 * STEP, lanes),
            half16(2, 8, PARTS * 8 * STEP, lanes),
            half16(2, 8, PARTS, 8 * STEP, lanes),
            half16(hids, PARTS, STEP, lanes),
            half16(chans, tall, lanes),
            pltpu.VMEM((chans * STEP, lanes), jnp.float32),
            pltpu.VMEM((2 * hids * STEP, lanes), jnp.float32),
            pltpu.VMEM((2, lanes, lanes), jnp.float32),
            pltpu.VMEM((4, lanes, lanes), jnp.float32),
            half16(4 * hids + chans, chans),
            half16(chans, hids),
            half16(hids, STEP, lanes),
            pltpu.VMEM((token_mask.shape[0] // lanes, lanes), jnp.int32),
            pltpu.VMEM((1, lanes), jnp.float32),
            pltpu.VMEM((1, lanes), jnp.float32),
            half16(*proj_in.shape),
            half16(*gate_in.shape),
            pltpu.VMEM((1, lanes), jnp.float32),
            pltpu.VMEM((1, lanes), jnp.float32),
            half16(*proj_out.shape),
            half16(*gate_out.shape),
            dma((6,)),
            dma((PARTS + 1,)),
            dma((PARTS,)),
            dma,
            dma,
            dma((ROUNDS,)),
            dma,
            dma((PARTS + 1,)),
            dma((PARTS,)),
            dma,
            dma((ROUNDS,)),
            dma,
            dma((9,)),
        ],
        compiler_params=pltpu.CompilerParams(
            collective_id=0, has_side_effects=True, vmem_limit_bytes=56 * 2**20
        ),
    )(
        pair,
        token_mask.reshape(-1, lanes),
        gain_in.reshape(1, -1),
        bias_in.reshape(1, -1),
        proj_in,
        gate_in,
        gain_out.reshape(1, -1),
        bias_out.reshape(1, -1),
        proj_out,
        gate_out,
    )


def solution(mesh):
    in_specs = (P("ch", "row", "col"),) + (P(),) * 9
    return jax.shard_map(local, mesh=mesh, in_specs=in_specs, out_specs=P("ch", "row", "col"), check_vma=False)
```

```python
import functools

import jax
import jax.numpy as jnp
from jax import lax
from jax.experimental import pallas as pl
from jax.experimental.pallas import tpu as pltpu
from jax.sharding import PartitionSpec as P

epsilon = 1e-05
MESH = pl.DeviceIdType.MESH
STEP = 16
PARTS = 4
ROUNDS = 4
PER = PARTS // ROUNDS
LANES = 128
SPARE = PARTS - 1
PEERS = 64


def mixed_order(offsets):
    def steps(offset):
        used = {"x": float(offset[0])}
        for name, hops in zip("yz", offset[1:3]):
            used[name + "+"] = float(hops in (1, 2))
            used[name + "-"] = float(hops in (2, 3))
        return used

    load = dict.fromkeys(("x", "y+", "y-", "z+", "z-"), 0.0)
    left, order = list(offsets), []
    while left:

        def score(offset):
            total = {k: v + steps(offset)[k] for k, v in load.items()}
            return max(total.values()) - min(total.values()), -sum(steps(offset).values())

        best = min(left, key=score)
        left.remove(best)
        order.append(best)
        load = {k: v + steps(best)[k] for k, v in load.items()}
    return order


CHIPS = [(n // 16, n // 4 % 4, n % 4) for n in range(1, 32)]
OTHERS = mixed_order([(0, 0, 0, 1)] + [c + (n,) for c in CHIPS for n in range(2)])
CHIPS = mixed_order(CHIPS)


def norm_rows(values, gain, bias):
    width = values.shape[0]
    center = jnp.sum(values, axis=0, keepdims=True) * (1.0 / width)
    second = jnp.sum(values * values, axis=0, keepdims=True) * (1.0 / width)
    spread = second - center * center
    return ((values - center) * lax.rsqrt(spread + epsilon) * gain + bias).astype(jnp.bfloat16)


def sigmoid(values):
    return 0.5 * jnp.tanh(0.5 * values) + 0.5


def part_rows(r):
    return pl.ds(pl.multiple_of(r * STEP, STEP), STEP)


def kernel(
    pair_ref,
    token_hbm,
    gain_in_hbm,
    bias_in_hbm,
    proj_in_hbm,
    gate_in_hbm,
    gain_out_hbm,
    bias_out_hbm,
    proj_out_hbm,
    gate_out_hbm,
    out_ref,
    pairs,
    hidden,
    gates,
    acts,
    far,
    tri,
    sums,
    result,
    flat,
    stage,
    mask,
    affine,
    weight_in,
    weight_out,
    extra,
    token_ref,
    gain_in_ref,
    bias_in_ref,
    proj_in_ref,
    gate_in_ref,
    gain_out_ref,
    bias_out_ref,
    proj_out_ref,
    gate_out_ref,
    send_sem,
    pair_sem,
    act_sem,
    extra_sem,
    far_sem,
    sum_sem,
    out_sem,
    own_pair_sem,
    own_act_sem,
    own_extra_sem,
    own_sum_sem,
    own_out_sem,
    small_sem,
):
    y, col, ch = lax.axis_index("row"), lax.axis_index("col"), lax.axis_index("ch")
    b, z = lax.div(col, 4), lax.rem(col, 4)
    low, core = lax.div(ch, 2), lax.rem(ch, 2)
    half = lax.rem(low + b, 2)
    quarter = half * 2 + core
    chan_part = pair_ref.shape[0]
    tall = STEP * PARTS

    def place(b2, y2, z2, core2):
        return {"row": y2, "col": b2 * 4 + z2, "ch": lax.rem(half + b2, 2) * 2 + core2}

    def group(b2, y2, z2, core2):
        return ((b2 * 4 + y2) * 4 + z2) * 2 + core2

    def peer(offset):
        return (
            lax.rem(b + offset[0], 2),
            lax.rem(y + offset[1], 4),
            lax.rem(z + offset[2], 4),
            lax.rem(core + offset[3], 2),
        )

    def across(core2):
        return {"row": y, "col": col, "ch": (1 - low) * 2 + core2}

    small = [
        pltpu.make_async_copy(src, dst, small_sem.at[n])
        for n, (src, dst) in enumerate(
            (
                (token_hbm, token_ref),
                (gain_in_hbm, gain_in_ref),
                (bias_in_hbm, bias_in_ref),
                (proj_in_hbm, proj_in_ref),
                (gate_in_hbm, gate_in_ref),
                (gain_out_hbm, gain_out_ref),
                (bias_out_hbm, bias_out_ref),
                (proj_out_hbm, proj_out_ref),
                (gate_out_hbm, gate_out_ref),
            )
        )
    ]
    for copy in small:
        copy.start()

    mine = group(b, y, z, core)
    spot = y * 2 + core

    barrier = pltpu.get_barrier_semaphore()

    for core2 in range(2):
        pl.semaphore_signal(barrier, inc=1, device_id=across(core2), device_id_type=MESH)
    for offset in OTHERS:
        pl.semaphore_signal(barrier, inc=1, device_id=place(*peer(offset)), device_id_type=MESH)
    pl.semaphore_wait(barrier, PEERS + 1)

    def rows_for(half2, core2, r):
        spare = lax.div(r, PARTS)
        half2 = lax.rem(half2 + spare, 2)
        return pl.ds(pl.multiple_of((half2 * 2 + core2) * tall + (r - spare) * STEP, STEP), STEP)

    def send_pairs(r, carry):
        for step in range(1, 4):
            ch2 = lax.rem(ch + step, 4)
            pltpu.make_async_remote_copy(
                src_ref=pair_ref.at[:, rows_for(lax.rem(lax.div(ch2, 2) + b, 2), lax.rem(ch2, 2), r), :],
                dst_ref=pairs.at[pl.ds(ch * chan_part, chan_part), part_rows(r), :],
                send_sem=send_sem.at[0],
                recv_sem=pair_sem.at[r],
                device_id={"row": y, "col": col, "ch": ch2},
                device_id_type=MESH,
            ).start()
        pltpu.make_async_copy(
            pair_ref.at[:, rows_for(half, core, r), :],
            pairs.at[pl.ds(ch * chan_part, chan_part), part_rows(r), :],
            own_pair_sem.at[r],
        ).start()
        return carry

    lax.fori_loop(0, PARTS + 1, send_pairs, 0)

    chans = pairs.shape[0]
    hids = hidden.shape[0]

    def turned(ref):
        return ref[...].astype(jnp.float32).T.astype(jnp.bfloat16)

    def column(vec):
        return jnp.broadcast_to(vec, (LANES, LANES)).T

    for copy in small:
        copy.wait()
    weight_in[: 2 * hids] = turned(gate_in_ref)
    weight_in[2 * hids : 4 * hids] = turned(proj_in_ref)
    weight_in[4 * hids :] = turned(gate_out_ref)
    weight_out[...] = turned(proj_out_ref)
    for n, ref in enumerate((gain_in_ref, bias_in_ref, gain_out_ref, bias_out_ref)):
        affine[n] = column(ref[...])
    for n in range(2):
        mask[n] = column(
            token_ref[pl.ds(y * 2 + lax.rem(half + n, 2), 1), :].astype(jnp.float32)
        ) * token_ref[pl.ds(col, 1), :].astype(jnp.float32)

    def take_pairs(r):
        held = pairs.at[pl.ds(0, 3 * chan_part), pl.ds(0, STEP), :]
        pltpu.make_async_copy(held, held, pair_sem.at[r]).wait()
        held = pairs.at[pl.ds(0, chan_part), pl.ds(0, STEP), :]
        pltpu.make_async_copy(held, held, own_pair_sem.at[r]).wait()
        flat[...] = pairs[:, part_rows(r), :].astype(jnp.float32).reshape(chans * STEP, LANES)

    def normed(i):
        both = [
            norm_rows(flat[pl.ds(i + d, chans, stride=STEP), :], affine[0], affine[1]) for d in range(2)
        ]
        return jnp.concatenate(both, axis=1)

    def make_hidden(r, carry):
        take_pairs(r)
        here_mask = mask[0, pl.ds(pl.multiple_of(core * tall + r * STEP, STEP), STEP), :]
        for i in range(0, STEP, 2):
            prod = jnp.dot(weight_in[...], normed(i), preferred_element_type=jnp.float32)
            for d in range(2):
                part = prod[:, d * LANES : (d + 1) * LANES]
                act = sigmoid(part[: 2 * hids]) * part[2 * hids : 4 * hids] * here_mask[i + d : i + d + 1, :]
                stage[pl.ds(i + d, 2 * hids, stride=STEP), :] = act
                gates[r * STEP + (i + d)] = sigmoid(part[4 * hids :])
        rounded = stage[...].astype(jnp.bfloat16).reshape(2, hids, STEP, LANES)
        hidden[:, 0, part_rows(r), :] = rounded[0]
        hidden[:, 1, part_rows(r), :] = rounded[1]
        here = pl.ds(pl.multiple_of(r * (8 * STEP) + spot * STEP, STEP), STEP)

        for offset in OTHERS:
            to = peer(offset)
            pltpu.make_async_remote_copy(
                src_ref=hidden.at[pl.ds(2 * group(*to), 2), :, part_rows(r), :],
                dst_ref=acts.at[:, :, col, here, :],
                send_sem=send_sem.at[1],
                recv_sem=act_sem.at[r],
                device_id=place(*to),
                device_id_type=MESH,
            ).start()
        pltpu.make_async_copy(
            hidden.at[pl.ds(2 * mine, 2), :, part_rows(r), :], acts.at[:, :, col, here, :], own_act_sem.at[r]
        ).start()
        return carry

    lax.fori_loop(0, PARTS, make_hidden, 0)

    def take_acts(r):
        held = hidden.at[pl.ds(0, 2 * PEERS - 2), :, pl.ds(0, STEP), :]
        pltpu.make_async_copy(held, held, act_sem.at[r]).wait()
        held = hidden.at[pl.ds(0, 2), :, pl.ds(0, STEP), :]
        pltpu.make_async_copy(held, held, own_act_sem.at[r]).wait()

    def pass_right(r):
        take_acts(r)
        rows = pl.ds(r * (8 * STEP), 8 * STEP)
        pltpu.make_async_remote_copy(
            src_ref=acts.at[:, 1, :, rows, :],
            dst_ref=far.at[:, :, rows, :],
            send_sem=send_sem.at[2],
            recv_sem=far_sem,
            device_id=across(core),
            device_id_type=MESH,
        ).start()

    pass_right(0)

    take_pairs(PARTS)
    spare_mask = mask[1, pl.ds(pl.multiple_of(core * tall + SPARE * STEP, STEP), STEP), :]
    for i in range(0, STEP, 2):
        both = normed(i)
        gate = jnp.dot(weight_in[hids : 2 * hids], both, preferred_element_type=jnp.float32)
        prod = jnp.dot(weight_in[3 * hids : 4 * hids], both, preferred_element_type=jnp.float32)
        for d in range(2):
            lanes = slice(d * LANES, (d + 1) * LANES)
            stage[pl.ds(i + d, hids, stride=STEP), :] = (
                sigmoid(gate[:, lanes]) * prod[:, lanes] * spare_mask[i + d : i + d + 1, :]
            )
    extra[...] = stage[pl.ds(0, hids * STEP), :].astype(jnp.bfloat16).reshape(hids, STEP, LANES)
    spare_rows = pl.ds(pl.multiple_of(SPARE * (8 * STEP) + spot * STEP, STEP), STEP)

    for offset in OTHERS:
        to = peer(offset)
        pltpu.make_async_remote_copy(
            src_ref=extra.at[pl.ds(2 * group(*to), 2)],
            dst_ref=far.at[:, col, spare_rows, :],
            send_sem=send_sem.at[5],
            recv_sem=extra_sem,
            device_id=place(*to),
            device_id_type=MESH,
        ).start()
    pltpu.make_async_copy(
        extra.at[pl.ds(2 * mine, 2)], far.at[:, col, spare_rows, :], own_extra_sem
    ).start()

    for r in range(1, SPARE):
        pass_right(r)
    take_acts(SPARE)

    def multiply(turn, start, parts, load_right):
        rows = pl.ds(start * (8 * STEP), parts * (8 * STEP))
        which = lax.rem(half + turn, 2)

        def block(n, carry):
            h, m = lax.div(n, 2), lax.rem(n, 2)
            left = jnp.concatenate([acts[h, 0, c, rows, :] for c in range(8)], axis=1)
            right = []
            for c in range(8):
                right.append(
                    jnp.concatenate(
                        [
                            load_right(h, c, pl.ds(pl.multiple_of(m * (4 * STEP) + (r * 8 + s) * STEP, STEP), STEP))
                            for s2 in range(2)
                            for s in (s2 * 2, s2 * 2 + 1)
                            for r in range(PARTS)
                        ],
                        axis=0,
                    )
                )
            prod = lax.dot_general(
                left,
                jnp.concatenate(right, axis=1),
                (((1,), (1,)), ((), ())),
                preferred_element_type=jnp.float32,
            ).astype(jnp.bfloat16)
            for s in range(2):
                tri[h, (m * 2 + s) * 2 + which, pl.ds(start, parts)] = prod[
                    :, s * LANES : (s + 1) * LANES
                ].reshape(parts, 8 * STEP, LANES)
            return carry

        lax.fori_loop(0, 4, block, 0)

    def send_round(n):
        part = pl.ds(n * PER, PER)

        def send_sums(b2, y2, z2, core2):
            pltpu.make_async_remote_copy(
                src_ref=tri.at[
                    :, b2 * 4 + z2, part, pl.ds(pl.multiple_of((y2 * 2 + core2) * STEP, STEP), STEP), :
                ],
                dst_ref=sums.at[pl.ds(2 * mine, 2), part],
                send_sem=send_sem.at[3],
                recv_sem=sum_sem.at[n],
                device_id=place(b2, y2, z2, core2),
                device_id_type=MESH,
            ).start()

        send_sums(b, y, z, 1 - core)
        pltpu.make_async_copy(
            tri.at[:, col, part, pl.ds(pl.multiple_of(spot * STEP, STEP), STEP), :],
            sums.at[pl.ds(2 * mine, 2), part],
            own_sum_sem.at[n],
        ).start()
        for core2 in range(2):
            for offset in CHIPS:
                send_sums(*peer(offset + (0,))[:3], core2)

    multiply(0, 0, PARTS, lambda h, c, rows: acts[h, 1, c, rows, :])
    held = extra.at[pl.ds(0, 2 * PEERS - 2)]
    pltpu.make_async_copy(held, held, extra_sem).wait()
    held = extra.at[pl.ds(0, 2)]
    pltpu.make_async_copy(held, held, own_extra_sem).wait()
    held = far.at[:, :, pl.ds(0, SPARE * 8 * STEP), :]
    pltpu.make_async_copy(held, held, far_sem).wait()
    for n in range(2):
        multiply(1, n * (PARTS // 2), PARTS // 2, lambda h, c, rows: far[h, c, rows, :])
        for m in range(n * (ROUNDS // 2), (n + 1) * (ROUNDS // 2)):
            send_round(m)

    def make_update(r, carry):
        flat[...] = sums[:, r].astype(jnp.float32).reshape(hids * STEP, LANES)
        for i in range(0, STEP, 2):
            both = [
                norm_rows(flat[pl.ds(i + d, hids, stride=STEP), :], affine[2], affine[3])
                for d in range(2)
            ]
            prod = jnp.dot(
                weight_out[...], jnp.concatenate(both, axis=1), preferred_element_type=jnp.float32
            )
            for d in range(2):
                stage[pl.ds(i + d, chans, stride=STEP), :] = (
                    gates[r * STEP + (i + d)] * prod[:, d * LANES : (d + 1) * LANES]
                )
        result[:, part_rows(r), :] = (
            stage[pl.ds(0, chans * STEP), :].astype(jnp.bfloat16).reshape(chans, STEP, LANES)
        )
        rows = pl.ds(pl.multiple_of(quarter * tall + r * STEP, STEP), STEP)
        for step in range(1, 4):
            ch2 = lax.rem(ch + step, 4)
            pltpu.make_async_remote_copy(
                src_ref=result.at[pl.ds(ch2 * chan_part, chan_part), part_rows(r), :],
                dst_ref=out_ref.at[:, rows, :],
                send_sem=send_sem.at[4],
                recv_sem=out_sem,
                device_id={"row": y, "col": col, "ch": ch2},
                device_id_type=MESH,
            ).start()
        pltpu.make_async_copy(
            result.at[pl.ds(ch * chan_part, chan_part), part_rows(r), :], out_ref.at[:, rows, :], own_out_sem
        ).start()
        return carry

    def take_round(n, carry):
        held = sums.at[pl.ds(0, 2 * PEERS - 2), pl.ds(0, PER)]
        pltpu.make_async_copy(held, held, sum_sem.at[n]).wait()
        held = sums.at[pl.ds(0, 2), pl.ds(0, PER)]
        pltpu.make_async_copy(held, held, own_sum_sem.at[n]).wait()
        lax.fori_loop(n * PER, n * PER + PER, make_update, 0)
        return carry

    lax.fori_loop(0, ROUNDS, take_round, 0)

    held = result.at[pl.ds(0, 3 * chan_part)]
    pltpu.make_async_copy(held, held, out_sem).wait()
    held = result.at[pl.ds(0, chan_part)]
    pltpu.make_async_copy(held, held, own_out_sem).wait()
    for n, held in enumerate(
        (
            pairs.at[pl.ds(0, 3 * chan_part)],
            hidden.at[pl.ds(0, 2 * PEERS - 2)],
            far.at[:, :, pl.ds(0, SPARE * 8 * STEP), :],
            sums.at[pl.ds(0, 2 * PEERS - 2)],
            result.at[pl.ds(0, 3 * chan_part)],
            extra.at[pl.ds(0, 2 * PEERS - 2)],
        )
    ):
        pltpu.make_async_copy(held, held, send_sem.at[n]).wait()


def local(pair, token_mask, gain_in, bias_in, proj_in, gate_in, gain_out, bias_out, proj_out, gate_out):
    chan_part, row_count, lanes = pair.shape
    chs = lax.axis_size("ch")
    chans, hids = chan_part * chs, proj_out.shape[0]
    tall = row_count // chs
    half16 = lambda *shape: pltpu.VMEM(shape, jnp.bfloat16)
    dma = pltpu.SemaphoreType.DMA
    return pl.pallas_call(
        kernel,
        name="update",
        out_shape=pltpu.VMEM(pair.shape, jnp.bfloat16),
        in_specs=[pl.BlockSpec(memory_space=pl.ANY)] + [pl.BlockSpec(memory_space=pl.ANY)] * 9,
        out_specs=pl.BlockSpec(memory_space=pl.ANY),
        scratch_shapes=[
            half16(chans, tall + STEP, lanes),
            half16(hids, 2, tall, lanes),
            pltpu.VMEM((tall, chans, lanes), jnp.float32),
            half16(2, 2, 8, PARTS * 8 * STEP, lanes),
            half16(2, 8, PARTS * 8 * STEP, lanes),
            half16(2, 8, PARTS, 8 * STEP, lanes),
            half16(hids, PARTS, STEP, lanes),
            half16(chans, tall, lanes),
            pltpu.VMEM((chans * STEP, lanes), jnp.float32),
            pltpu.VMEM((2 * hids * STEP, lanes), jnp.float32),
            pltpu.VMEM((2, lanes, lanes), jnp.float32),
            pltpu.VMEM((4, lanes, lanes), jnp.float32),
            half16(4 * hids + chans, chans),
            half16(chans, hids),
            half16(hids, STEP, lanes),
            pltpu.VMEM((token_mask.shape[0] // lanes, lanes), jnp.int32),
            pltpu.VMEM((1, lanes), jnp.float32),
            pltpu.VMEM((1, lanes), jnp.float32),
            half16(*proj_in.shape),
            half16(*gate_in.shape),
            pltpu.VMEM((1, lanes), jnp.float32),
            pltpu.VMEM((1, lanes), jnp.float32),
            half16(*proj_out.shape),
            half16(*gate_out.shape),
            dma((6,)),
            dma((PARTS + 1,)),
            dma((PARTS,)),
            dma,
            dma,
            dma((ROUNDS,)),
            dma,
            dma((PARTS + 1,)),
            dma((PARTS,)),
            dma,
            dma((ROUNDS,)),
            dma,
            dma((9,)),
        ],
        compiler_params=pltpu.CompilerParams(
            collective_id=0, has_side_effects=True, vmem_limit_bytes=56 * 2**20
        ),
    )(
        pair,
        token_mask.reshape(-1, lanes),
        gain_in.reshape(1, -1),
        bias_in.reshape(1, -1),
        proj_in,
        gate_in,
        gain_out.reshape(1, -1),
        bias_out.reshape(1, -1),
        proj_out,
        gate_out,
    )


def solution(mesh):
    in_specs = (P("ch", "row", "col"),) + (P(),) * 9
    return jax.shard_map(local, mesh=mesh, in_specs=in_specs, out_specs=P("ch", "row", "col"), check_vma=False)
```

```python
import functools

import jax
import jax.numpy as jnp
from jax import lax
from jax.experimental import pallas as pl
from jax.experimental.pallas import tpu as pltpu
from jax.sharding import PartitionSpec as P

epsilon = 1e-05
MESH = pl.DeviceIdType.MESH
STEP = 16
PARTS = 4
AHEAD = 2
LANES = 128
SPARE = PARTS - 1
PEERS = 64


def mixed_order(offsets):
    def steps(offset):
        used = {"x": float(offset[0])}
        for name, hops in zip("yz", offset[1:3]):
            used[name + "+"] = float(hops in (1, 2))
            used[name + "-"] = float(hops in (2, 3))
        return used

    load = dict.fromkeys(("x", "y+", "y-", "z+", "z-"), 0.0)
    left, order = list(offsets), []
    while left:

        def score(offset):
            total = {k: v + steps(offset)[k] for k, v in load.items()}
            return max(total.values()) - min(total.values()), -sum(steps(offset).values())

        best = min(left, key=score)
        left.remove(best)
        order.append(best)
        load = {k: v + steps(best)[k] for k, v in load.items()}
    return order


CHIPS = [(n // 16, n // 4 % 4, n % 4) for n in range(1, 32)]
OTHERS = mixed_order([(0, 0, 0, 1)] + [c + (n,) for c in CHIPS for n in range(2)])
CHIPS = mixed_order(CHIPS)


def norm_rows(values, gain, bias):
    width = values.shape[0]
    center = jnp.sum(values, axis=0, keepdims=True) * (1.0 / width)
    second = jnp.sum(values * values, axis=0, keepdims=True) * (1.0 / width)
    spread = second - center * center
    return ((values - center) * lax.rsqrt(spread + epsilon) * gain + bias).astype(jnp.bfloat16)


def twice_sigmoid(half_values):
    return jnp.tanh(half_values) + 1.0


def part_rows(r):
    return pl.ds(pl.multiple_of(r * STEP, STEP), STEP)


def kernel(
    pair_ref,
    token_hbm,
    gain_in_hbm,
    bias_in_hbm,
    proj_in_hbm,
    gate_in_hbm,
    gain_out_hbm,
    bias_out_hbm,
    proj_out_hbm,
    gate_out_hbm,
    out_ref,
    pairs,
    hidden,
    gates,
    acts,
    far,
    tri,
    sums,
    result,
    flat,
    stage,
    mask,
    affine,
    weight_in,
    weight_out,
    ready,
    extra,
    token_ref,
    gain_in_ref,
    bias_in_ref,
    proj_in_ref,
    gate_in_ref,
    gain_out_ref,
    bias_out_ref,
    proj_out_ref,
    gate_out_ref,
    send_sem,
    pair_sem,
    act_sem,
    extra_sem,
    far_sem,
    sum_sem,
    out_sem,
    own_pair_sem,
    own_act_sem,
    own_extra_sem,
    own_sum_sem,
    own_out_sem,
    small_sem,
):
    y, col, ch = lax.axis_index("row"), lax.axis_index("col"), lax.axis_index("ch")
    b, z = lax.div(col, 4), lax.rem(col, 4)
    low, core = lax.div(ch, 2), lax.rem(ch, 2)
    half = lax.rem(low + b, 2)
    quarter = half * 2 + core
    chan_part = pair_ref.shape[0]
    tall = STEP * PARTS

    def place(b2, y2, z2, core2):
        return {"row": y2, "col": b2 * 4 + z2, "ch": lax.rem(half + b2, 2) * 2 + core2}

    def group(b2, y2, z2, core2):
        return ((b2 * 4 + y2) * 4 + z2) * 2 + core2

    def peer(offset):
        return (
            lax.rem(b + offset[0], 2),
            lax.rem(y + offset[1], 4),
            lax.rem(z + offset[2], 4),
            lax.rem(core + offset[3], 2),
        )

    def across(core2):
        return {"row": y, "col": col, "ch": (1 - low) * 2 + core2}

    small = [
        pltpu.make_async_copy(src, dst, small_sem.at[n])
        for n, (src, dst) in enumerate(
            (
                (token_hbm, token_ref),
                (gain_in_hbm, gain_in_ref),
                (bias_in_hbm, bias_in_ref),
                (proj_in_hbm, proj_in_ref),
                (gate_in_hbm, gate_in_ref),
                (gain_out_hbm, gain_out_ref),
                (bias_out_hbm, bias_out_ref),
                (proj_out_hbm, proj_out_ref),
                (gate_out_hbm, gate_out_ref),
            )
        )
    ]
    mine = group(b, y, z, core)
    spot = y * 2 + core

    barrier = pltpu.get_barrier_semaphore()

    for core2 in range(2):
        pl.semaphore_signal(barrier, inc=1, device_id=across(core2), device_id_type=MESH)
    for offset in OTHERS:
        pl.semaphore_signal(barrier, inc=1, device_id=place(*peer(offset)), device_id_type=MESH)
    for copy in small:
        copy.start()
    pl.semaphore_wait(barrier, PEERS + 1)

    def rows_for(half2, core2, r):
        spare = lax.div(r, PARTS)
        half2 = lax.rem(half2 + spare, 2)
        return pl.ds(pl.multiple_of((half2 * 2 + core2) * tall + (r - spare) * STEP, STEP), STEP)

    def send_pairs(r, carry):
        for step in range(1, 4):
            ch2 = lax.rem(ch + step, 4)
            pltpu.make_async_remote_copy(
                src_ref=pair_ref.at[:, rows_for(lax.rem(lax.div(ch2, 2) + b, 2), lax.rem(ch2, 2), r), :],
                dst_ref=pairs.at[pl.ds(ch * chan_part, chan_part), part_rows(r), :],
                send_sem=send_sem.at[0],
                recv_sem=pair_sem.at[r],
                device_id={"row": y, "col": col, "ch": ch2},
                device_id_type=MESH,
            ).start()
        pltpu.make_async_copy(
            pair_ref.at[:, rows_for(half, core, r), :],
            pairs.at[pl.ds(ch * chan_part, chan_part), part_rows(r), :],
            own_pair_sem.at[r],
        ).start()
        return carry

    lax.fori_loop(0, PARTS + 1, send_pairs, 0)

    chans = pairs.shape[0]
    hids = hidden.shape[1]

    def turned(ref, scale=1.0):
        return (ref[...].astype(jnp.float32).T * scale).astype(jnp.bfloat16)

    def column(vec):
        return jnp.broadcast_to(vec, (LANES, LANES)).T

    for copy in small:
        copy.wait()
    weight_in[: 2 * hids] = turned(gate_in_ref, 0.5)
    weight_in[2 * hids : 4 * hids] = turned(proj_in_ref)
    weight_in[4 * hids :] = turned(gate_out_ref, 0.5)
    weight_out[...] = turned(proj_out_ref, 0.5)
    for n, ref in enumerate((gain_in_ref, bias_in_ref, gain_out_ref, bias_out_ref)):
        affine[n] = column(ref[...])
    for n in range(2):
        mask[n] = column(
            token_ref[pl.ds(y * 2 + lax.rem(half + n, 2), 1), :].astype(jnp.float32)
        ) * (token_ref[pl.ds(col, 1), :].astype(jnp.float32) * 0.5)

    def take_pairs(r):
        held = pairs.at[pl.ds(0, 3 * chan_part), pl.ds(0, STEP), :]
        pltpu.make_async_copy(held, held, pair_sem.at[r]).wait()
        held = pairs.at[pl.ds(0, chan_part), pl.ds(0, STEP), :]
        pltpu.make_async_copy(held, held, own_pair_sem.at[r]).wait()
        flat[...] = pairs[:, part_rows(r), :].astype(jnp.float32).reshape(chans * STEP, LANES)

    def normed(i):
        both = [
            norm_rows(flat[pl.ds(i + d, chans, stride=STEP), :], affine[0], affine[1]) for d in range(2)
        ]
        return jnp.concatenate(both, axis=1)

    def take_acts(r):
        held = hidden.at[0, pl.ds(0, 2 * PEERS - 2)]
        pltpu.make_async_copy(held, held, act_sem.at[r]).wait()
        held = hidden.at[0, pl.ds(0, 2)]
        pltpu.make_async_copy(held, held, own_act_sem.at[r]).wait()

    def pass_right(r):
        take_acts(r)
        rows = pl.ds(r * (8 * STEP), 8 * STEP)
        pltpu.make_async_remote_copy(
            src_ref=acts.at[:, 1, :, rows, :],
            dst_ref=far.at[:, :, rows, :],
            send_sem=send_sem.at[2],
            recv_sem=far_sem,
            device_id=across(core),
            device_id_type=MESH,
        ).start()

    def make_hidden(r, carry):
        take_pairs(r)
        here_mask = mask[0, pl.ds(pl.multiple_of(core * tall + r * STEP, STEP), STEP), :]
        for i in range(0, STEP, 2):
            prod = jnp.dot(weight_in[...], normed(i), preferred_element_type=jnp.float32)
            for d in range(2):
                part = prod[:, d * LANES : (d + 1) * LANES]
                act = twice_sigmoid(part[: 2 * hids]) * part[2 * hids : 4 * hids] * here_mask[i + d : i + d + 1, :]
                stage[pl.ds(i + d, 2 * hids, stride=STEP), :] = act
                gates[r * STEP + (i + d)] = twice_sigmoid(part[4 * hids :])
        rounded = stage[...].astype(jnp.bfloat16).reshape(2, hids, STEP, LANES)
        hidden[r, :, 0] = rounded[0]
        hidden[r, :, 1] = rounded[1]
        here = pl.ds(pl.multiple_of(r * (8 * STEP) + spot * STEP, STEP), STEP)

        @pl.when(r == PARTS - 1)
        def _():
            pass_right(0)


        for offset in OTHERS:
            to = peer(offset)
            pltpu.make_async_remote_copy(
                src_ref=hidden.at[r, pl.ds(2 * group(*to), 2)],
                dst_ref=acts.at[:, :, col, here, :],
                send_sem=send_sem.at[1],
                recv_sem=act_sem.at[r],
                device_id=place(*to),
                device_id_type=MESH,
            ).start()
        pltpu.make_async_copy(
            hidden.at[r, pl.ds(2 * mine, 2)], acts.at[:, :, col, here, :], own_act_sem.at[r]
        ).start()
        return carry

    lax.fori_loop(0, PARTS, make_hidden, 0)

    take_pairs(PARTS)
    spare_mask = mask[1, pl.ds(pl.multiple_of(core * tall + SPARE * STEP, STEP), STEP), :]
    for i in range(0, STEP, 2):
        both = normed(i)
        gate = jnp.dot(weight_in[hids : 2 * hids], both, preferred_element_type=jnp.float32)
        prod = jnp.dot(weight_in[3 * hids : 4 * hids], both, preferred_element_type=jnp.float32)
        for d in range(2):
            lanes = slice(d * LANES, (d + 1) * LANES)
            stage[pl.ds(i + d, hids, stride=STEP), :] = (
                twice_sigmoid(gate[:, lanes]) * prod[:, lanes] * spare_mask[i + d : i + d + 1, :]
            )
    extra[...] = stage[pl.ds(0, hids * STEP), :].astype(jnp.bfloat16).reshape(hids, STEP, LANES)
    spare_rows = pl.ds(pl.multiple_of(SPARE * (8 * STEP) + spot * STEP, STEP), STEP)

    for offset in OTHERS:
        to = peer(offset)
        pltpu.make_async_remote_copy(
            src_ref=extra.at[pl.ds(2 * group(*to), 2)],
            dst_ref=far.at[:, col, spare_rows, :],
            send_sem=send_sem.at[5],
            recv_sem=extra_sem,
            device_id=place(*to),
            device_id_type=MESH,
        ).start()
    pltpu.make_async_copy(
        extra.at[pl.ds(2 * mine, 2)], far.at[:, col, spare_rows, :], own_extra_sem
    ).start()

    for r in range(1, SPARE):
        pass_right(r)
    take_acts(SPARE)

    def multiply(turn, start, parts, load_right):
        rows = pl.ds(start * (8 * STEP), parts * (8 * STEP))
        which = lax.rem(half + turn, 2)

        def block(n, carry):
            h, m = lax.div(n, 2), lax.rem(n, 2)
            left = jnp.concatenate([acts[h, 0, c, rows, :] for c in range(8)], axis=1)
            right = []
            for c in range(8):
                right.append(
                    jnp.concatenate(
                        [
                            load_right(h, c, pl.ds(pl.multiple_of(m * (4 * STEP) + (r * 8 + s) * STEP, STEP), STEP))
                            for s2 in range(2)
                            for s in (s2 * 2, s2 * 2 + 1)
                            for r in range(PARTS)
                        ],
                        axis=0,
                    )
                )
            prod = lax.dot_general(
                left,
                jnp.concatenate(right, axis=1),
                (((1,), (1,)), ((), ())),
                preferred_element_type=jnp.float32,
            ).astype(jnp.bfloat16)
            for s in range(2):
                tri[(m * 2 + s) * 2 + which, pl.ds(start, parts), :, h] = prod[
                    :, s * LANES : (s + 1) * LANES
                ].reshape(parts, 8, STEP, LANES)
            return carry

        lax.fori_loop(0, 4, block, 0)

    def send_round(n):
        def send_sums(b2, y2, z2, core2):
            pltpu.make_async_remote_copy(
                src_ref=tri.at[b2 * 4 + z2, n, y2 * 2 + core2],
                dst_ref=sums.at[n, pl.ds(2 * mine, 2)],
                send_sem=send_sem.at[3],
                recv_sem=sum_sem.at[n],
                device_id=place(b2, y2, z2, core2),
                device_id_type=MESH,
            ).start()

        send_sums(b, y, z, 1 - core)
        pltpu.make_async_copy(
            tri.at[col, n, spot],
            sums.at[n, pl.ds(2 * mine, 2)],
            own_sum_sem.at[n],
        ).start()
        for core2 in range(2):
            for offset in CHIPS:
                send_sums(*peer(offset + (0,))[:3], core2)

    multiply(0, 0, PARTS, lambda h, c, rows: acts[h, 1, c, rows, :])
    held = extra.at[pl.ds(0, 2 * PEERS - 2)]
    pltpu.make_async_copy(held, held, extra_sem).wait()
    held = extra.at[pl.ds(0, 2)]
    pltpu.make_async_copy(held, held, own_extra_sem).wait()
    held = far.at[:, :, pl.ds(0, SPARE * 8 * STEP), :]
    pltpu.make_async_copy(held, held, far_sem).wait()
    for n in range(2):
        multiply(1, n * (PARTS // 2), PARTS // 2, lambda h, c, rows: far[h, c, rows, :])
        send_round(n)

    def make_update(r, carry):
        held = sums.at[0, pl.ds(0, 2 * PEERS - 2)]
        pltpu.make_async_copy(held, held, sum_sem.at[r]).wait()
        held = sums.at[0, pl.ds(0, 2)]
        pltpu.make_async_copy(held, held, own_sum_sem.at[r]).wait()
        flat[...] = sums[r].astype(jnp.float32).reshape(hids * STEP, LANES)
        for i in range(0, STEP, 2):
            both = [
                norm_rows(flat[pl.ds(i + d, hids, stride=STEP), :], affine[2], affine[3])
                for d in range(2)
            ]
            ready[i // 2] = jnp.concatenate(both, axis=1)
        rows = pl.ds(pl.multiple_of(quarter * tall + r * STEP, STEP), STEP)
        share = chans // 2
        for chip in (1 - low, low):
            here = pl.ds(pl.multiple_of(chip * share, share), share)
            weight = weight_out[here, :]
            for i in range(0, STEP, 2):
                prod = jnp.dot(weight, ready[i // 2], preferred_element_type=jnp.float32)
                for d in range(2):
                    stage[pl.ds(i + d, share, stride=STEP), :] = (
                        gates[r * STEP + (i + d), here, :] * prod[:, d * LANES : (d + 1) * LANES]
                    )
            result[here, part_rows(r), :] = (
                stage[pl.ds(0, share * STEP), :].astype(jnp.bfloat16).reshape(share, STEP, LANES)
            )
            first = chip is not low
            for core2 in (0, 1) if first else (1 - core,):
                ch2 = chip * 2 + core2
                pltpu.make_async_remote_copy(
                    src_ref=result.at[pl.ds(ch2 * chan_part, chan_part), part_rows(r), :],
                    dst_ref=out_ref.at[:, rows, :],
                    send_sem=send_sem.at[4],
                    recv_sem=out_sem,
                    device_id={"row": y, "col": col, "ch": ch2},
                    device_id_type=MESH,
                ).start()
        pltpu.make_async_copy(
            result.at[pl.ds(ch * chan_part, chan_part), part_rows(r), :], out_ref.at[:, rows, :], own_out_sem
        ).start()

        @pl.when(r + AHEAD < PARTS)
        def _():
            send_round(r + AHEAD)

        return carry

    lax.fori_loop(0, PARTS, make_update, 0)

    held = result.at[pl.ds(0, 3 * chan_part)]
    pltpu.make_async_copy(held, held, out_sem).wait()
    held = result.at[pl.ds(0, chan_part)]
    pltpu.make_async_copy(held, held, own_out_sem).wait()
    for n, held in enumerate(
        (
            pairs.at[pl.ds(0, 3 * chan_part)],
            hidden.at[:, pl.ds(0, 2 * PEERS - 2)],
            far.at[:, :, pl.ds(0, SPARE * 8 * STEP), :],
            sums.at[:, pl.ds(0, 2 * PEERS - 2)],
            result.at[pl.ds(0, 3 * chan_part)],
            extra.at[pl.ds(0, 2 * PEERS - 2)],
        )
    ):
        pltpu.make_async_copy(held, held, send_sem.at[n]).wait()


def local(pair, token_mask, gain_in, bias_in, proj_in, gate_in, gain_out, bias_out, proj_out, gate_out):
    chan_part, row_count, lanes = pair.shape
    chs = lax.axis_size("ch")
    chans, hids = chan_part * chs, proj_out.shape[0]
    tall = row_count // chs
    half16 = lambda *shape: pltpu.VMEM(shape, jnp.bfloat16)
    dma = pltpu.SemaphoreType.DMA
    return pl.pallas_call(
        kernel,
        name="update",
        out_shape=pltpu.VMEM(pair.shape, jnp.bfloat16),
        in_specs=[pl.BlockSpec(memory_space=pl.ANY)] + [pl.BlockSpec(memory_space=pl.ANY)] * 9,
        out_specs=pl.BlockSpec(memory_space=pl.ANY),
        scratch_shapes=[
            half16(chans, tall + STEP, lanes),
            half16(PARTS, hids, 2, STEP, lanes),
            pltpu.VMEM((tall, chans, lanes), jnp.float32),
            half16(2, 2, 8, PARTS * 8 * STEP, lanes),
            half16(2, 8, PARTS * 8 * STEP, lanes),
            half16(8, PARTS, 8, 2, STEP, lanes),
            half16(PARTS, hids, STEP, lanes),
            half16(chans, tall, lanes),
            pltpu.VMEM((chans * STEP, lanes), jnp.float32),
            pltpu.VMEM((2 * hids * STEP, lanes), jnp.float32),
            pltpu.VMEM((2, lanes, lanes), jnp.float32),
            pltpu.VMEM((4, lanes, lanes), jnp.float32),
            half16(4 * hids + chans, chans),
            half16(chans, hids),
            half16(STEP // 2, hids, 2 * lanes),
            half16(hids, STEP, lanes),
            pltpu.VMEM((token_mask.shape[0] // lanes, lanes), jnp.int32),
            pltpu.VMEM((1, lanes), jnp.float32),
            pltpu.VMEM((1, lanes), jnp.float32),
            half16(*proj_in.shape),
            half16(*gate_in.shape),
            pltpu.VMEM((1, lanes), jnp.float32),
            pltpu.VMEM((1, lanes), jnp.float32),
            half16(*proj_out.shape),
            half16(*gate_out.shape),
            dma((6,)),
            dma((PARTS + 1,)),
            dma((PARTS,)),
            dma,
            dma,
            dma((PARTS,)),
            dma,
            dma((PARTS + 1,)),
            dma((PARTS,)),
            dma,
            dma((PARTS,)),
            dma,
            dma((9,)),
        ],
        compiler_params=pltpu.CompilerParams(
            collective_id=0, has_side_effects=True, vmem_limit_bytes=56 * 2**20
        ),
    )(
        pair,
        token_mask.reshape(-1, lanes),
        gain_in.reshape(1, -1),
        bias_in.reshape(1, -1),
        proj_in,
        gate_in,
        gain_out.reshape(1, -1),
        bias_out.reshape(1, -1),
        proj_out,
        gate_out,
    )


def solution(mesh):
    in_specs = (P("ch", "row", "col"),) + (P(),) * 9
    return jax.shard_map(local, mesh=mesh, in_specs=in_specs, out_specs=P("ch", "row", "col"), check_vma=False)
```

```python
import functools

import jax
import jax.numpy as jnp
from jax import lax
from jax.experimental import pallas as pl
from jax.experimental.pallas import tpu as pltpu
from jax.sharding import PartitionSpec as P

epsilon = 1e-05
MESH = pl.DeviceIdType.MESH
STEP = 16
PARTS = 4
AHEAD = 2
LANES = 128
SPARE = PARTS - 1
PEERS = 64


def mixed_order(offsets):
    def steps(offset):
        used = {"x": float(offset[0])}
        for name, hops in zip("yz", offset[1:3]):
            used[name + "+"] = float(hops in (1, 2))
            used[name + "-"] = float(hops in (2, 3))
        return used

    load = dict.fromkeys(("x", "y+", "y-", "z+", "z-"), 0.0)
    left, order = list(offsets), []
    while left:

        def score(offset):
            total = {k: v + steps(offset)[k] for k, v in load.items()}
            return max(total.values()) - min(total.values()), -sum(steps(offset).values())

        best = min(left, key=score)
        left.remove(best)
        order.append(best)
        load = {k: v + steps(best)[k] for k, v in load.items()}
    return order


CHIPS = [(n // 16, n // 4 % 4, n % 4) for n in range(1, 32)]
OTHERS = mixed_order([(0, 0, 0, 1)] + [c + (n,) for c in CHIPS for n in range(2)])
CHIPS = mixed_order(CHIPS)


def norm_rows(values, gain, bias):
    width = values.shape[0]
    center = jnp.sum(values, axis=0, keepdims=True) * (1.0 / width)
    second = jnp.sum(values * values, axis=0, keepdims=True) * (1.0 / width)
    spread = second - center * center
    return ((values - center) * lax.rsqrt(spread + epsilon) * gain + bias).astype(jnp.bfloat16)


def twice_sigmoid(half_values):
    return jnp.tanh(half_values) + 1.0


def part_rows(r):
    return pl.ds(pl.multiple_of(r * STEP, STEP), STEP)


def kernel(
    pair_ref,
    token_hbm,
    gain_in_hbm,
    bias_in_hbm,
    proj_in_hbm,
    gate_in_hbm,
    gain_out_hbm,
    bias_out_hbm,
    proj_out_hbm,
    gate_out_hbm,
    out_ref,
    pairs,
    hidden,
    gates,
    acts,
    far,
    tri,
    sums,
    result,
    flat,
    stage,
    mask,
    affine,
    weight_in,
    weight_out,
    ready,
    extra,
    token_ref,
    gain_in_ref,
    bias_in_ref,
    proj_in_ref,
    gate_in_ref,
    gain_out_ref,
    bias_out_ref,
    proj_out_ref,
    gate_out_ref,
    send_sem,
    pair_sem,
    act_sem,
    extra_sem,
    far_sem,
    sum_sem,
    out_sem,
    own_pair_sem,
    own_act_sem,
    own_extra_sem,
    own_sum_sem,
    own_out_sem,
    small_sem,
):
    y, col, ch = lax.axis_index("row"), lax.axis_index("col"), lax.axis_index("ch")
    b, z = lax.div(col, 4), lax.rem(col, 4)
    low, core = lax.div(ch, 2), lax.rem(ch, 2)
    half = lax.rem(low + b, 2)
    quarter = half * 2 + core
    chan_part = pair_ref.shape[0]
    tall = STEP * PARTS

    def place(b2, y2, z2, core2):
        return {"row": y2, "col": b2 * 4 + z2, "ch": lax.rem(half + b2, 2) * 2 + core2}

    def group(b2, y2, z2, core2):
        return ((b2 * 4 + y2) * 4 + z2) * 2 + core2

    def peer(offset):
        return (
            lax.rem(b + offset[0], 2),
            lax.rem(y + offset[1], 4),
            lax.rem(z + offset[2], 4),
            lax.rem(core + offset[3], 2),
        )

    def across(core2):
        return {"row": y, "col": col, "ch": (1 - low) * 2 + core2}

    small = [
        pltpu.make_async_copy(src, dst, small_sem.at[n])
        for n, (src, dst) in enumerate(
            (
                (token_hbm, token_ref),
                (gain_in_hbm, gain_in_ref),
                (bias_in_hbm, bias_in_ref),
                (proj_in_hbm, proj_in_ref),
                (gate_in_hbm, gate_in_ref),
                (gain_out_hbm, gain_out_ref),
                (bias_out_hbm, bias_out_ref),
                (proj_out_hbm, proj_out_ref),
                (gate_out_hbm, gate_out_ref),
            )
        )
    ]
    mine = group(b, y, z, core)
    spot = y * 2 + core

    barrier = pltpu.get_barrier_semaphore()

    for core2 in range(2):
        pl.semaphore_signal(barrier, inc=1, device_id=across(core2), device_id_type=MESH)
    for offset in OTHERS:
        pl.semaphore_signal(barrier, inc=1, device_id=place(*peer(offset)), device_id_type=MESH)
    for copy in small:
        copy.start()
    pl.semaphore_wait(barrier, PEERS + 1)

    def rows_for(half2, core2, r):
        spare = lax.div(r, PARTS)
        half2 = lax.rem(half2 + spare, 2)
        return pl.ds(pl.multiple_of((half2 * 2 + core2) * tall + (r - spare) * STEP, STEP), STEP)

    def send_pairs(r, carry):
        for step in range(1, 4):
            ch2 = lax.rem(ch + step, 4)
            pltpu.make_async_remote_copy(
                src_ref=pair_ref.at[:, rows_for(lax.rem(lax.div(ch2, 2) + b, 2), lax.rem(ch2, 2), r), :],
                dst_ref=pairs.at[pl.ds(ch * chan_part, chan_part), part_rows(r), :],
                send_sem=send_sem.at[0],
                recv_sem=pair_sem.at[r],
                device_id={"row": y, "col": col, "ch": ch2},
                device_id_type=MESH,
            ).start()
        pltpu.make_async_copy(
            pair_ref.at[:, rows_for(half, core, r), :],
            pairs.at[pl.ds(ch * chan_part, chan_part), part_rows(r), :],
            own_pair_sem.at[r],
        ).start()
        return carry

    lax.fori_loop(0, PARTS + 1, send_pairs, 0)

    chans = pairs.shape[0]
    hids = hidden.shape[1]

    def turned(ref, scale=1.0):
        return (ref[...].astype(jnp.float32).T * scale).astype(jnp.bfloat16)

    def column(vec):
        return jnp.broadcast_to(vec, (LANES, LANES)).T

    for copy in small:
        copy.wait()
    weight_in[: 2 * hids] = turned(gate_in_ref, 0.5)
    weight_in[2 * hids : 4 * hids] = turned(proj_in_ref)
    weight_in[4 * hids :] = turned(gate_out_ref, 0.5)
    weight_out[...] = turned(proj_out_ref, 0.5)
    for n, ref in enumerate((gain_in_ref, bias_in_ref, gain_out_ref, bias_out_ref)):
        affine[n] = column(ref[...])
    for n in range(2):
        mask[n] = column(
            token_ref[pl.ds(y * 2 + lax.rem(half + n, 2), 1), :].astype(jnp.float32)
        ) * (token_ref[pl.ds(col, 1), :].astype(jnp.float32) * 0.5)

    def take_pairs(r):
        held = pairs.at[pl.ds(0, 3 * chan_part), pl.ds(0, STEP), :]
        pltpu.make_async_copy(held, held, pair_sem.at[r]).wait()
        held = pairs.at[pl.ds(0, chan_part), pl.ds(0, STEP), :]
        pltpu.make_async_copy(held, held, own_pair_sem.at[r]).wait()
        flat[...] = pairs[:, part_rows(r), :].astype(jnp.float32).reshape(chans * STEP, LANES)

    def normed(i):
        both = [
            norm_rows(flat[pl.ds(i + d, chans, stride=STEP), :], affine[0], affine[1]) for d in range(2)
        ]
        return jnp.concatenate(both, axis=1)

    def take_acts(r):
        held = hidden.at[0, pl.ds(0, 2 * PEERS - 2)]
        pltpu.make_async_copy(held, held, act_sem.at[r]).wait()
        held = hidden.at[0, pl.ds(0, 2)]
        pltpu.make_async_copy(held, held, own_act_sem.at[r]).wait()

    def pass_right(r):
        take_acts(r)
        rows = pl.ds(r * (8 * STEP), 8 * STEP)
        pltpu.make_async_remote_copy(
            src_ref=acts.at[:, 1, :, rows, :],
            dst_ref=far.at[:, :, rows, :],
            send_sem=send_sem.at[2],
            recv_sem=far_sem,
            device_id=across(core),
            device_id_type=MESH,
        ).start()

    def make_hidden(r, carry):
        take_pairs(r)
        here_mask = mask[0, pl.ds(pl.multiple_of(core * tall + r * STEP, STEP), STEP), :]
        for i in range(0, STEP, 2):
            prod = jnp.dot(weight_in[...], normed(i), preferred_element_type=jnp.float32)
            for d in range(2):
                part = prod[:, d * LANES : (d + 1) * LANES]
                act = twice_sigmoid(part[: 2 * hids]) * part[2 * hids : 4 * hids] * here_mask[i + d : i + d + 1, :]
                stage[pl.ds(i + d, 2 * hids, stride=STEP), :] = act
                gates[r * STEP + (i + d)] = twice_sigmoid(part[4 * hids :])
        rounded = stage[...].astype(jnp.bfloat16).reshape(2, hids, STEP, LANES)
        hidden[r, :, 0] = rounded[0]
        hidden[r, :, 1] = rounded[1]
        here = pl.ds(pl.multiple_of(r * (8 * STEP) + spot * STEP, STEP), STEP)

        @pl.when(r == PARTS - 1)
        def _():
            pass_right(0)


        for offset in OTHERS:
            to = peer(offset)
            pltpu.make_async_remote_copy(
                src_ref=hidden.at[r, pl.ds(2 * group(*to), 2)],
                dst_ref=acts.at[:, :, col, here, :],
                send_sem=send_sem.at[1],
                recv_sem=act_sem.at[r],
                device_id=place(*to),
                device_id_type=MESH,
            ).start()
        pltpu.make_async_copy(
            hidden.at[r, pl.ds(2 * mine, 2)], acts.at[:, :, col, here, :], own_act_sem.at[r]
        ).start()
        return carry

    lax.fori_loop(0, PARTS, make_hidden, 0)

    take_pairs(PARTS)
    spare_mask = mask[1, pl.ds(pl.multiple_of(core * tall + SPARE * STEP, STEP), STEP), :]
    for i in range(0, STEP, 2):
        both = normed(i)
        gate = jnp.dot(weight_in[hids : 2 * hids], both, preferred_element_type=jnp.float32)
        prod = jnp.dot(weight_in[3 * hids : 4 * hids], both, preferred_element_type=jnp.float32)
        for d in range(2):
            lanes = slice(d * LANES, (d + 1) * LANES)
            stage[pl.ds(i + d, hids, stride=STEP), :] = (
                twice_sigmoid(gate[:, lanes]) * prod[:, lanes] * spare_mask[i + d : i + d + 1, :]
            )
    extra[...] = stage[pl.ds(0, hids * STEP), :].astype(jnp.bfloat16).reshape(hids, STEP, LANES)
    spare_rows = pl.ds(pl.multiple_of(SPARE * (8 * STEP) + spot * STEP, STEP), STEP)

    for offset in OTHERS:
        to = peer(offset)
        pltpu.make_async_remote_copy(
            src_ref=extra.at[pl.ds(2 * group(*to), 2)],
            dst_ref=far.at[:, col, spare_rows, :],
            send_sem=send_sem.at[5],
            recv_sem=extra_sem,
            device_id=place(*to),
            device_id_type=MESH,
        ).start()
    pltpu.make_async_copy(
        extra.at[pl.ds(2 * mine, 2)], far.at[:, col, spare_rows, :], own_extra_sem
    ).start()

    for r in range(1, SPARE):
        pass_right(r)
    take_acts(SPARE)

    def multiply(turn, start, parts, load_right):
        rows = pl.ds(start * (8 * STEP), parts * (8 * STEP))
        which = lax.rem(half + turn, 2)

        def block(n, carry):
            h, m = lax.div(n, 2), lax.rem(n, 2)
            left = jnp.concatenate([acts[h, 0, c, rows, :] for c in range(8)], axis=1)
            right = []
            for c in range(8):
                right.append(
                    jnp.concatenate(
                        [
                            load_right(h, c, pl.ds(pl.multiple_of(m * (4 * STEP) + (r * 8 + s) * STEP, STEP), STEP))
                            for s2 in range(2)
                            for s in (s2 * 2, s2 * 2 + 1)
                            for r in range(PARTS)
                        ],
                        axis=0,
                    )
                )
            prod = lax.dot_general(
                left,
                jnp.concatenate(right, axis=1),
                (((1,), (1,)), ((), ())),
                preferred_element_type=jnp.float32,
            ).astype(jnp.bfloat16)
            for s in range(2):
                tri[(m * 2 + s) * 2 + which, pl.ds(start, parts), :, h] = prod[
                    :, s * LANES : (s + 1) * LANES
                ].reshape(parts, 8, STEP, LANES)
            return carry

        lax.fori_loop(0, 4, block, 0)

    def send_round(n):
        def send_sums(b2, y2, z2, core2):
            pltpu.make_async_remote_copy(
                src_ref=tri.at[b2 * 4 + z2, n, y2 * 2 + core2],
                dst_ref=sums.at[n, pl.ds(2 * mine, 2)],
                send_sem=send_sem.at[3],
                recv_sem=sum_sem.at[n],
                device_id=place(b2, y2, z2, core2),
                device_id_type=MESH,
            ).start()

        send_sums(b, y, z, 1 - core)
        pltpu.make_async_copy(
            tri.at[col, n, spot],
            sums.at[n, pl.ds(2 * mine, 2)],
            own_sum_sem.at[n],
        ).start()
        for core2 in range(2):
            for offset in CHIPS:
                send_sums(*peer(offset + (0,))[:3], core2)

    multiply(0, 0, PARTS, lambda h, c, rows: acts[h, 1, c, rows, :])
    held = extra.at[pl.ds(0, 2 * PEERS - 2)]
    pltpu.make_async_copy(held, held, extra_sem).wait()
    held = extra.at[pl.ds(0, 2)]
    pltpu.make_async_copy(held, held, own_extra_sem).wait()
    held = far.at[:, :, pl.ds(0, SPARE * 8 * STEP), :]
    pltpu.make_async_copy(held, held, far_sem).wait()
    for n, parts in enumerate((1, PARTS - 1)):
        multiply(1, n, parts, lambda h, c, rows: far[h, c, rows, :])
        send_round(n)

    def make_update(r, carry):
        held = sums.at[0, pl.ds(0, 2 * PEERS - 2)]
        pltpu.make_async_copy(held, held, sum_sem.at[r]).wait()
        held = sums.at[0, pl.ds(0, 2)]
        pltpu.make_async_copy(held, held, own_sum_sem.at[r]).wait()
        flat[...] = sums[r].astype(jnp.float32).reshape(hids * STEP, LANES)
        for i in range(0, STEP, 2):
            both = [
                norm_rows(flat[pl.ds(i + d, hids, stride=STEP), :], affine[2], affine[3])
                for d in range(2)
            ]
            ready[i // 2] = jnp.concatenate(both, axis=1)
        rows = pl.ds(pl.multiple_of(quarter * tall + r * STEP, STEP), STEP)
        share = chans // 2
        for chip in (1 - low, low):
            here = pl.ds(pl.multiple_of(chip * share, share), share)
            weight = weight_out[here, :]
            for i in range(0, STEP, 2):
                prod = jnp.dot(weight, ready[i // 2], preferred_element_type=jnp.float32)
                for d in range(2):
                    stage[pl.ds(i + d, share, stride=STEP), :] = (
                        gates[r * STEP + (i + d), here, :] * prod[:, d * LANES : (d + 1) * LANES]
                    )
            result[here, part_rows(r), :] = (
                stage[pl.ds(0, share * STEP), :].astype(jnp.bfloat16).reshape(share, STEP, LANES)
            )
            first = chip is not low
            for core2 in (0, 1) if first else (1 - core,):
                ch2 = chip * 2 + core2
                pltpu.make_async_remote_copy(
                    src_ref=result.at[pl.ds(ch2 * chan_part, chan_part), part_rows(r), :],
                    dst_ref=out_ref.at[:, rows, :],
                    send_sem=send_sem.at[4],
                    recv_sem=out_sem,
                    device_id={"row": y, "col": col, "ch": ch2},
                    device_id_type=MESH,
                ).start()
        pltpu.make_async_copy(
            result.at[pl.ds(ch * chan_part, chan_part), part_rows(r), :], out_ref.at[:, rows, :], own_out_sem
        ).start()

        @pl.when(r + AHEAD < PARTS)
        def _():
            send_round(r + AHEAD)

        return carry

    lax.fori_loop(0, PARTS, make_update, 0)

    held = result.at[pl.ds(0, 3 * chan_part)]
    pltpu.make_async_copy(held, held, out_sem).wait()
    held = result.at[pl.ds(0, chan_part)]
    pltpu.make_async_copy(held, held, own_out_sem).wait()
    for n, held in enumerate(
        (
            pairs.at[pl.ds(0, 3 * chan_part)],
            hidden.at[:, pl.ds(0, 2 * PEERS - 2)],
            far.at[:, :, pl.ds(0, SPARE * 8 * STEP), :],
            sums.at[:, pl.ds(0, 2 * PEERS - 2)],
            result.at[pl.ds(0, 3 * chan_part)],
            extra.at[pl.ds(0, 2 * PEERS - 2)],
        )
    ):
        pltpu.make_async_copy(held, held, send_sem.at[n]).wait()


def local(pair, token_mask, gain_in, bias_in, proj_in, gate_in, gain_out, bias_out, proj_out, gate_out):
    chan_part, row_count, lanes = pair.shape
    chs = lax.axis_size("ch")
    chans, hids = chan_part * chs, proj_out.shape[0]
    tall = row_count // chs
    half16 = lambda *shape: pltpu.VMEM(shape, jnp.bfloat16)
    dma = pltpu.SemaphoreType.DMA
    return pl.pallas_call(
        kernel,
        name="update",
        out_shape=pltpu.VMEM(pair.shape, jnp.bfloat16),
        in_specs=[pl.BlockSpec(memory_space=pl.ANY)] + [pl.BlockSpec(memory_space=pl.ANY)] * 9,
        out_specs=pl.BlockSpec(memory_space=pl.ANY),
        scratch_shapes=[
            half16(chans, tall + STEP, lanes),
            half16(PARTS, hids, 2, STEP, lanes),
            pltpu.VMEM((tall, chans, lanes), jnp.float32),
            half16(2, 2, 8, PARTS * 8 * STEP, lanes),
            half16(2, 8, PARTS * 8 * STEP, lanes),
            half16(8, PARTS, 8, 2, STEP, lanes),
            half16(PARTS, hids, STEP, lanes),
            half16(chans, tall, lanes),
            pltpu.VMEM((chans * STEP, lanes), jnp.float32),
            pltpu.VMEM((2 * hids * STEP, lanes), jnp.float32),
            pltpu.VMEM((2, lanes, lanes), jnp.float32),
            pltpu.VMEM((4, lanes, lanes), jnp.float32),
            half16(4 * hids + chans, chans),
            half16(chans, hids),
            half16(STEP // 2, hids, 2 * lanes),
            half16(hids, STEP, lanes),
            pltpu.VMEM((token_mask.shape[0] // lanes, lanes), jnp.int32),
            pltpu.VMEM((1, lanes), jnp.float32),
            pltpu.VMEM((1, lanes), jnp.float32),
            half16(*proj_in.shape),
            half16(*gate_in.shape),
            pltpu.VMEM((1, lanes), jnp.float32),
            pltpu.VMEM((1, lanes), jnp.float32),
            half16(*proj_out.shape),
            half16(*gate_out.shape),
            dma((6,)),
            dma((PARTS + 1,)),
            dma((PARTS,)),
            dma,
            dma,
            dma((PARTS,)),
            dma,
            dma((PARTS + 1,)),
            dma((PARTS,)),
            dma,
            dma((PARTS,)),
            dma,
            dma((9,)),
        ],
        compiler_params=pltpu.CompilerParams(
            collective_id=0, has_side_effects=True, vmem_limit_bytes=56 * 2**20
        ),
    )(
        pair,
        token_mask.reshape(-1, lanes),
        gain_in.reshape(1, -1),
        bias_in.reshape(1, -1),
        proj_in,
        gate_in,
        gain_out.reshape(1, -1),
        bias_out.reshape(1, -1),
        proj_out,
        gate_out,
    )


def solution(mesh):
    in_specs = (P("ch", "row", "col"),) + (P(),) * 9
    return jax.shard_map(local, mesh=mesh, in_specs=in_specs, out_specs=P("ch", "row", "col"), check_vma=False)
```

```python
import functools

import jax
import jax.numpy as jnp
from jax import lax
from jax.experimental import pallas as pl
from jax.experimental.pallas import tpu as pltpu
from jax.sharding import PartitionSpec as P

epsilon = 1e-05
MESH = pl.DeviceIdType.MESH
STEP = 16
PARTS = 4
AHEAD = 3
LANES = 128
SPARE = PARTS - 1
PEERS = 64


def mixed_order(offsets):
    def steps(offset):
        used = {"x": float(offset[0])}
        for name, hops in zip("yz", offset[1:3]):
            used[name + "+"] = float(hops in (1, 2))
            used[name + "-"] = float(hops in (2, 3))
        return used

    load = dict.fromkeys(("x", "y+", "y-", "z+", "z-"), 0.0)
    left, order = list(offsets), []
    while left:

        def score(offset):
            total = {k: v + steps(offset)[k] for k, v in load.items()}
            return max(total.values()) - min(total.values()), -sum(steps(offset).values())

        best = min(left, key=score)
        left.remove(best)
        order.append(best)
        load = {k: v + steps(best)[k] for k, v in load.items()}
    return order


CHIPS = [(n // 16, n // 4 % 4, n % 4) for n in range(1, 32)]
OTHERS = mixed_order([(0, 0, 0, 1)] + [c + (n,) for c in CHIPS for n in range(2)])
CHIPS = mixed_order(CHIPS)


def norm_rows(values, gain, bias):
    width = values.shape[0]
    center = jnp.sum(values, axis=0, keepdims=True) * (1.0 / width)
    second = jnp.sum(values * values, axis=0, keepdims=True) * (1.0 / width)
    spread = second - center * center
    return ((values - center) * lax.rsqrt(spread + epsilon) * gain + bias).astype(jnp.bfloat16)


def twice_sigmoid(half_values):
    return jnp.tanh(half_values) + 1.0


def part_rows(r):
    return pl.ds(pl.multiple_of(r * STEP, STEP), STEP)


def kernel(
    pair_ref,
    token_hbm,
    gain_in_hbm,
    bias_in_hbm,
    proj_in_hbm,
    gate_in_hbm,
    gain_out_hbm,
    bias_out_hbm,
    proj_out_hbm,
    gate_out_hbm,
    out_ref,
    pairs,
    hidden,
    gates,
    acts,
    far,
    tri,
    sums,
    result,
    flat,
    stage,
    mask,
    affine,
    weight_in,
    weight_out,
    ready,
    extra,
    token_ref,
    gain_in_ref,
    bias_in_ref,
    proj_in_ref,
    gate_in_ref,
    gain_out_ref,
    bias_out_ref,
    proj_out_ref,
    gate_out_ref,
    send_sem,
    pair_sem,
    act_sem,
    extra_sem,
    far_sem,
    sum_sem,
    out_sem,
    own_pair_sem,
    own_act_sem,
    own_extra_sem,
    own_sum_sem,
    own_out_sem,
    small_sem,
):
    y, col, ch = lax.axis_index("row"), lax.axis_index("col"), lax.axis_index("ch")
    b, z = lax.div(col, 4), lax.rem(col, 4)
    low, core = lax.div(ch, 2), lax.rem(ch, 2)
    half = lax.rem(low + b, 2)
    quarter = half * 2 + core
    chan_part = pair_ref.shape[0]
    tall = STEP * PARTS

    def place(b2, y2, z2, core2):
        return {"row": y2, "col": b2 * 4 + z2, "ch": lax.rem(half + b2, 2) * 2 + core2}

    def group(b2, y2, z2, core2):
        return ((b2 * 4 + y2) * 4 + z2) * 2 + core2

    def peer(offset):
        return (
            lax.rem(b + offset[0], 2),
            lax.rem(y + offset[1], 4),
            lax.rem(z + offset[2], 4),
            lax.rem(core + offset[3], 2),
        )

    def across(core2):
        return {"row": y, "col": col, "ch": (1 - low) * 2 + core2}

    small = [
        pltpu.make_async_copy(src, dst, small_sem.at[n])
        for n, (src, dst) in enumerate(
            (
                (token_hbm, token_ref),
                (gain_in_hbm, gain_in_ref),
                (bias_in_hbm, bias_in_ref),
                (proj_in_hbm, proj_in_ref),
                (gate_in_hbm, gate_in_ref),
                (gain_out_hbm, gain_out_ref),
                (bias_out_hbm, bias_out_ref),
                (proj_out_hbm, proj_out_ref),
                (gate_out_hbm, gate_out_ref),
            )
        )
    ]
    mine = group(b, y, z, core)
    spot = y * 2 + core

    barrier = pltpu.get_barrier_semaphore()

    for core2 in range(2):
        pl.semaphore_signal(barrier, inc=1, device_id=across(core2), device_id_type=MESH)
    for offset in OTHERS:
        pl.semaphore_signal(barrier, inc=1, device_id=place(*peer(offset)), device_id_type=MESH)
    for copy in small:
        copy.start()
    pl.semaphore_wait(barrier, PEERS + 1)

    def rows_for(half2, core2, r):
        spare = lax.div(r, PARTS)
        half2 = lax.rem(half2 + spare, 2)
        return pl.ds(pl.multiple_of((half2 * 2 + core2) * tall + (r - spare) * STEP, STEP), STEP)

    def send_pairs(r, carry):
        for step in range(1, 4):
            ch2 = lax.rem(ch + step, 4)
            pltpu.make_async_remote_copy(
                src_ref=pair_ref.at[:, rows_for(lax.rem(lax.div(ch2, 2) + b, 2), lax.rem(ch2, 2), r), :],
                dst_ref=pairs.at[pl.ds(ch * chan_part, chan_part), part_rows(r), :],
                send_sem=send_sem.at[0],
                recv_sem=pair_sem.at[r],
                device_id={"row": y, "col": col, "ch": ch2},
                device_id_type=MESH,
            ).start()
        pltpu.make_async_copy(
            pair_ref.at[:, rows_for(half, core, r), :],
            pairs.at[pl.ds(ch * chan_part, chan_part), part_rows(r), :],
            own_pair_sem.at[r],
        ).start()
        return carry

    lax.fori_loop(0, PARTS + 1, send_pairs, 0)

    chans = pairs.shape[0]
    hids = hidden.shape[1]

    def turned(ref, scale=1.0):
        return (ref[...].astype(jnp.float32).T * scale).astype(jnp.bfloat16)

    def column(vec):
        return jnp.broadcast_to(vec, (LANES, LANES)).T

    for copy in small:
        copy.wait()
    weight_in[: 2 * hids] = turned(gate_in_ref, 0.5)
    weight_in[2 * hids : 4 * hids] = turned(proj_in_ref)
    weight_in[4 * hids :] = turned(gate_out_ref, 0.5)
    weight_out[...] = turned(proj_out_ref, 0.5)
    for n, ref in enumerate((gain_in_ref, bias_in_ref, gain_out_ref, bias_out_ref)):
        affine[n] = column(ref[...])
    for n in range(2):
        mask[n] = column(
            token_ref[pl.ds(y * 2 + lax.rem(half + n, 2), 1), :].astype(jnp.float32)
        ) * (token_ref[pl.ds(col, 1), :].astype(jnp.float32) * 0.5)

    def take_pairs(r):
        held = pairs.at[pl.ds(0, 3 * chan_part), pl.ds(0, STEP), :]
        pltpu.make_async_copy(held, held, pair_sem.at[r]).wait()
        held = pairs.at[pl.ds(0, chan_part), pl.ds(0, STEP), :]
        pltpu.make_async_copy(held, held, own_pair_sem.at[r]).wait()
        flat[...] = pairs[:, part_rows(r), :].astype(jnp.float32).reshape(chans * STEP, LANES)

    def normed(i):
        both = [
            norm_rows(flat[pl.ds(i + d, chans, stride=STEP), :], affine[0], affine[1]) for d in range(2)
        ]
        return jnp.concatenate(both, axis=1)

    def take_acts(r):
        held = hidden.at[0, pl.ds(0, 2 * PEERS - 2)]
        pltpu.make_async_copy(held, held, act_sem.at[r]).wait()
        held = hidden.at[0, pl.ds(0, 2)]
        pltpu.make_async_copy(held, held, own_act_sem.at[r]).wait()

    def pass_right(r):
        take_acts(r)
        rows = pl.ds(r * (8 * STEP), 8 * STEP)
        pltpu.make_async_remote_copy(
            src_ref=acts.at[:, 1, :, rows, :],
            dst_ref=far.at[:, :, rows, :],
            send_sem=send_sem.at[2],
            recv_sem=far_sem,
            device_id=across(core),
            device_id_type=MESH,
        ).start()

    def make_hidden(r, carry):
        take_pairs(r)
        here_mask = mask[0, pl.ds(pl.multiple_of(core * tall + r * STEP, STEP), STEP), :]
        for i in range(0, STEP, 2):
            prod = jnp.dot(weight_in[...], normed(i), preferred_element_type=jnp.float32)
            for d in range(2):
                part = prod[:, d * LANES : (d + 1) * LANES]
                act = twice_sigmoid(part[: 2 * hids]) * part[2 * hids : 4 * hids] * here_mask[i + d : i + d + 1, :]
                stage[pl.ds(i + d, 2 * hids, stride=STEP), :] = act
                gates[r * STEP + (i + d)] = twice_sigmoid(part[4 * hids :])
        rounded = stage[...].astype(jnp.bfloat16).reshape(2, hids, STEP, LANES)
        hidden[r, :, 0] = rounded[0]
        hidden[r, :, 1] = rounded[1]
        here = pl.ds(pl.multiple_of(r * (8 * STEP) + spot * STEP, STEP), STEP)

        @pl.when(r == PARTS - 1)
        def _():
            pass_right(0)


        for offset in OTHERS:
            to = peer(offset)
            pltpu.make_async_remote_copy(
                src_ref=hidden.at[r, pl.ds(2 * group(*to), 2)],
                dst_ref=acts.at[:, :, col, here, :],
                send_sem=send_sem.at[1],
                recv_sem=act_sem.at[r],
                device_id=place(*to),
                device_id_type=MESH,
            ).start()
        pltpu.make_async_copy(
            hidden.at[r, pl.ds(2 * mine, 2)], acts.at[:, :, col, here, :], own_act_sem.at[r]
        ).start()
        return carry

    lax.fori_loop(0, PARTS, make_hidden, 0)

    take_pairs(PARTS)
    spare_mask = mask[1, pl.ds(pl.multiple_of(core * tall + SPARE * STEP, STEP), STEP), :]
    for i in range(0, STEP, 2):
        both = normed(i)
        gate = jnp.dot(weight_in[hids : 2 * hids], both, preferred_element_type=jnp.float32)
        prod = jnp.dot(weight_in[3 * hids : 4 * hids], both, preferred_element_type=jnp.float32)
        for d in range(2):
            lanes = slice(d * LANES, (d + 1) * LANES)
            stage[pl.ds(i + d, hids, stride=STEP), :] = (
                twice_sigmoid(gate[:, lanes]) * prod[:, lanes] * spare_mask[i + d : i + d + 1, :]
            )
    extra[...] = stage[pl.ds(0, hids * STEP), :].astype(jnp.bfloat16).reshape(hids, STEP, LANES)
    spare_rows = pl.ds(pl.multiple_of(SPARE * (8 * STEP) + spot * STEP, STEP), STEP)

    for offset in OTHERS:
        to = peer(offset)
        pltpu.make_async_remote_copy(
            src_ref=extra.at[pl.ds(2 * group(*to), 2)],
            dst_ref=far.at[:, col, spare_rows, :],
            send_sem=send_sem.at[5],
            recv_sem=extra_sem,
            device_id=place(*to),
            device_id_type=MESH,
        ).start()
    pltpu.make_async_copy(
        extra.at[pl.ds(2 * mine, 2)], far.at[:, col, spare_rows, :], own_extra_sem
    ).start()

    for r in range(1, SPARE):
        pass_right(r)
    take_acts(SPARE)

    def multiply(turn, start, parts, load_right):
        rows = pl.ds(start * (8 * STEP), parts * (8 * STEP))
        which = lax.rem(half + turn, 2)

        def block(n, carry):
            h, m = lax.div(n, 2), lax.rem(n, 2)
            left = jnp.concatenate([acts[h, 0, c, rows, :] for c in range(8)], axis=1)
            right = []
            for c in range(8):
                right.append(
                    jnp.concatenate(
                        [
                            load_right(h, c, pl.ds(pl.multiple_of(m * (4 * STEP) + (r * 8 + s) * STEP, STEP), STEP))
                            for s2 in range(2)
                            for s in (s2 * 2, s2 * 2 + 1)
                            for r in range(PARTS)
                        ],
                        axis=0,
                    )
                )
            prod = lax.dot_general(
                left,
                jnp.concatenate(right, axis=1),
                (((1,), (1,)), ((), ())),
                preferred_element_type=jnp.float32,
            ).astype(jnp.bfloat16)
            for s in range(2):
                tri[(m * 2 + s) * 2 + which, pl.ds(start, parts), :, h] = prod[
                    :, s * LANES : (s + 1) * LANES
                ].reshape(parts, 8, STEP, LANES)
            return carry

        lax.fori_loop(0, 4, block, 0)

    def send_round(n):
        def send_sums(b2, y2, z2, core2):
            pltpu.make_async_remote_copy(
                src_ref=tri.at[b2 * 4 + z2, n, y2 * 2 + core2],
                dst_ref=sums.at[n, pl.ds(2 * mine, 2)],
                send_sem=send_sem.at[3],
                recv_sem=sum_sem.at[n],
                device_id=place(b2, y2, z2, core2),
                device_id_type=MESH,
            ).start()

        send_sums(b, y, z, 1 - core)
        pltpu.make_async_copy(
            tri.at[col, n, spot],
            sums.at[n, pl.ds(2 * mine, 2)],
            own_sum_sem.at[n],
        ).start()
        for core2 in range(2):
            for offset in CHIPS:
                send_sums(*peer(offset + (0,))[:3], core2)

    multiply(0, 0, PARTS, lambda h, c, rows: acts[h, 1, c, rows, :])
    held = extra.at[pl.ds(0, 2 * PEERS - 2)]
    pltpu.make_async_copy(held, held, extra_sem).wait()
    held = extra.at[pl.ds(0, 2)]
    pltpu.make_async_copy(held, held, own_extra_sem).wait()
    held = far.at[:, :, pl.ds(0, SPARE * 8 * STEP), :]
    pltpu.make_async_copy(held, held, far_sem).wait()
    for n in range(2):
        multiply(1, n * (PARTS // 2), PARTS // 2, lambda h, c, rows: far[h, c, rows, :])
        send_round(n)
    send_round(AHEAD - 1)

    def make_update(r, carry):
        held = sums.at[0, pl.ds(0, 2 * PEERS - 2)]
        pltpu.make_async_copy(held, held, sum_sem.at[r]).wait()
        held = sums.at[0, pl.ds(0, 2)]
        pltpu.make_async_copy(held, held, own_sum_sem.at[r]).wait()
        flat[...] = sums[r].astype(jnp.float32).reshape(hids * STEP, LANES)
        for i in range(0, STEP, 2):
            both = [
                norm_rows(flat[pl.ds(i + d, hids, stride=STEP), :], affine[2], affine[3])
                for d in range(2)
            ]
            ready[i // 2] = jnp.concatenate(both, axis=1)
        rows = pl.ds(pl.multiple_of(quarter * tall + r * STEP, STEP), STEP)
        share = chans // 2
        for chip in (1 - low, low):
            here = pl.ds(pl.multiple_of(chip * share, share), share)
            weight = weight_out[here, :]
            for i in range(0, STEP, 2):
                prod = jnp.dot(weight, ready[i // 2], preferred_element_type=jnp.float32)
                for d in range(2):
                    stage[pl.ds(i + d, share, stride=STEP), :] = (
                        gates[r * STEP + (i + d), here, :] * prod[:, d * LANES : (d + 1) * LANES]
                    )
            result[here, part_rows(r), :] = (
                stage[pl.ds(0, share * STEP), :].astype(jnp.bfloat16).reshape(share, STEP, LANES)
            )
            first = chip is not low
            for core2 in (0, 1) if first else (1 - core,):
                ch2 = chip * 2 + core2
                pltpu.make_async_remote_copy(
                    src_ref=result.at[pl.ds(ch2 * chan_part, chan_part), part_rows(r), :],
                    dst_ref=out_ref.at[:, rows, :],
                    send_sem=send_sem.at[4],
                    recv_sem=out_sem,
                    device_id={"row": y, "col": col, "ch": ch2},
                    device_id_type=MESH,
                ).start()
        pltpu.make_async_copy(
            result.at[pl.ds(ch * chan_part, chan_part), part_rows(r), :], out_ref.at[:, rows, :], own_out_sem
        ).start()

        @pl.when(r + AHEAD < PARTS)
        def _():
            send_round(r + AHEAD)

        return carry

    lax.fori_loop(0, PARTS, make_update, 0)

    held = result.at[pl.ds(0, 3 * chan_part)]
    pltpu.make_async_copy(held, held, out_sem).wait()
    held = result.at[pl.ds(0, chan_part)]
    pltpu.make_async_copy(held, held, own_out_sem).wait()
    for n, held in enumerate(
        (
            pairs.at[pl.ds(0, 3 * chan_part)],
            hidden.at[:, pl.ds(0, 2 * PEERS - 2)],
            far.at[:, :, pl.ds(0, SPARE * 8 * STEP), :],
            sums.at[:, pl.ds(0, 2 * PEERS - 2)],
            result.at[pl.ds(0, 3 * chan_part)],
            extra.at[pl.ds(0, 2 * PEERS - 2)],
        )
    ):
        pltpu.make_async_copy(held, held, send_sem.at[n]).wait()


def local(pair, token_mask, gain_in, bias_in, proj_in, gate_in, gain_out, bias_out, proj_out, gate_out):
    chan_part, row_count, lanes = pair.shape
    chs = lax.axis_size("ch")
    chans, hids = chan_part * chs, proj_out.shape[0]
    tall = row_count // chs
    half16 = lambda *shape: pltpu.VMEM(shape, jnp.bfloat16)
    dma = pltpu.SemaphoreType.DMA
    return pl.pallas_call(
        kernel,
        name="update",
        out_shape=pltpu.VMEM(pair.shape, jnp.bfloat16),
        in_specs=[pl.BlockSpec(memory_space=pl.ANY)] + [pl.BlockSpec(memory_space=pl.ANY)] * 9,
        out_specs=pl.BlockSpec(memory_space=pl.ANY),
        scratch_shapes=[
            half16(chans, tall + STEP, lanes),
            half16(PARTS, hids, 2, STEP, lanes),
            pltpu.VMEM((tall, chans, lanes), jnp.float32),
            half16(2, 2, 8, PARTS * 8 * STEP, lanes),
            half16(2, 8, PARTS * 8 * STEP, lanes),
            half16(8, PARTS, 8, 2, STEP, lanes),
            half16(PARTS, hids, STEP, lanes),
            half16(chans, tall, lanes),
            pltpu.VMEM((chans * STEP, lanes), jnp.float32),
            pltpu.VMEM((2 * hids * STEP, lanes), jnp.float32),
            pltpu.VMEM((2, lanes, lanes), jnp.float32),
            pltpu.VMEM((4, lanes, lanes), jnp.float32),
            half16(4 * hids + chans, chans),
            half16(chans, hids),
            half16(STEP // 2, hids, 2 * lanes),
            half16(hids, STEP, lanes),
            pltpu.VMEM((token_mask.shape[0] // lanes, lanes), jnp.int32),
            pltpu.VMEM((1, lanes), jnp.float32),
            pltpu.VMEM((1, lanes), jnp.float32),
            half16(*proj_in.shape),
            half16(*gate_in.shape),
            pltpu.VMEM((1, lanes), jnp.float32),
            pltpu.VMEM((1, lanes), jnp.float32),
            half16(*proj_out.shape),
            half16(*gate_out.shape),
            dma((6,)),
            dma((PARTS + 1,)),
            dma((PARTS,)),
            dma,
            dma,
            dma((PARTS,)),
            dma,
            dma((PARTS + 1,)),
            dma((PARTS,)),
            dma,
            dma((PARTS,)),
            dma,
            dma((9,)),
        ],
        compiler_params=pltpu.CompilerParams(
            collective_id=0, has_side_effects=True, vmem_limit_bytes=56 * 2**20
        ),
    )(
        pair,
        token_mask.reshape(-1, lanes),
        gain_in.reshape(1, -1),
        bias_in.reshape(1, -1),
        proj_in,
        gate_in,
        gain_out.reshape(1, -1),
        bias_out.reshape(1, -1),
        proj_out,
        gate_out,
    )


def solution(mesh):
    in_specs = (P("ch", "row", "col"),) + (P(),) * 9
    return jax.shard_map(local, mesh=mesh, in_specs=in_specs, out_specs=P("ch", "row", "col"), check_vma=False)
```
